256 devices in a mesh: seq: 32 (over z, x), head: 8 (over y, core).
Axes of the slice: x: 4, y: 4, z: 8, core: 2. Of those that a mesh axis runs over, the one named last changes fastest.
Arguments:
- tokens: bfloat16 [32768, 1024], P(('seq', 'head')), may hold values from -6 to 6
- win_first: int32 [32768], P('seq'), may hold values from 0 to 32767, as said below
- win_count: int32 [32768], P('seq'), may hold values from 1 to 64, as said below
- norm1_gain: float32 [1024], replicated, may hold values from 0.25 to 1.75
- qkv_weight: bfloat16 [1024, 3, 1024], P('seq', None, 'head'), may hold values from -0.1875 to 0.1875
- qk_gain: float32 [2, 16, 64], P(None, 'head'), may hold values from 0.25 to 1.75
- out_weight: bfloat16 [1024, 1024], P('head', 'seq'), may hold values from -0.1875 to 0.1875
- norm2_gain: float32 [1024], replicated, may hold values from 0.25 to 1.75
- up_weight: bfloat16 [1024, 4096], P('seq', 'head'), may hold values from -0.1875 to 0.1875
- down_weight: bfloat16 [4096, 1024], P('head', 'seq'), may hold values from -0.09375 to 0.09375
Outputs:
- block_out: bfloat16 [32768, 1024], P(('seq', 'head'))
The draws below stay inside these ranges and needn't reach their ends.
Inputs may be any that keep to these rules, and one draw needn't show every extreme that they name: Each token's window block is the run of consecutive tokens from win_first to win_first + win_count - 1, which contains the token; window blocks tile the tokens in order, and some window block has exactly 64 tokens. `win_count`: all tokens of one window block carry the same count.
All inputs are finite; a program needn't handle non-finite values.
Results may differ from the reference program's by a relative error of at most 0.008.
Values may be sent and summed in bfloat16 or wider, within the bound.
No kernel may reach another device: no remote copies, remote signals or barrier semaphores. Data moves between devices by JAX's collectives and lax.ppermute only.
A program may use at most 64 MiB of HBM per device.

```python
import math
import jax
import jax.numpy as jnp
from jax import lax

D = 1024
HEADS = 16
HD = 64
FF = 4096
WIN_MOST = 64
TOKENS = 32768


def window_table(key):
    base = jax.random.fold_in(key, 7)
    length_key, forced_key = jax.random.split(base)
    lengths = jax.random.randint(length_key, (TOKENS,), 1, WIN_MOST + 1, dtype=jnp.int32)
    forced = jax.random.randint(forced_key, (), 0, min(32, TOKENS // WIN_MOST), dtype=jnp.int32)
    positions = jnp.arange(TOKENS, dtype=jnp.int32)
    lengths = jnp.where(positions == forced, jnp.int32(WIN_MOST), lengths)
    ends = jnp.cumsum(lengths).astype(jnp.int32)
    starts = ends - lengths
    owner = jnp.searchsorted(ends, positions, side='right').astype(jnp.int32)
    first = starts[owner]
    count = jnp.minimum(lengths[owner], jnp.int32(TOKENS) - first)
    return (first.astype(jnp.int32), count.astype(jnp.int32))


def draw_win_first(key, part):
    return window_table(key)[0]


def draw_win_count(key, part):
    return window_table(key)[1]


def shard_levels(key, shape, cuts, low, top_value):
    level = 1.0
    for position, shards_of in cuts:
        draws = jax.random.uniform(jax.random.fold_in(jax.random.fold_in(key, 6), position), (shards_of,), jnp.float32, low / len(cuts), top_value / len(cuts))
        level = level * jnp.repeat(jnp.exp(draws), shape[position] // shards_of).reshape((-1,) + (1,) * (len(shape) - 1 - position))
    return level


def normal_values(key, extent, scale, bound, shards=(), kind=jnp.bfloat16):
    entries = jax.random.normal(key, extent, jnp.float32) * scale
    if len(shards) > 0:
        entries = shard_levels(key, extent, shards, -0.22, 0.18) * entries
    return jnp.clip(entries, min=-bound, max=bound).astype(kind)


def setup_inputs(seed: int = 0) -> dict:
    key_of = jax.random.split(jax.random.key(seed), 11)
    tokens = normal_values(key_of[0], (TOKENS, D), 1.0, 6.0, ((0, 256),))
    win_first = draw_win_first(jax.random.fold_in(key_of[10], 71), 0)
    win_count = draw_win_count(jax.random.fold_in(key_of[10], 71), 0)
    norm1_gain = jnp.clip(1.0 + 0.15 * jax.random.normal(key_of[3], (D,), jnp.float32), 0.25, 1.75)
    qkv_weight = normal_values(key_of[4], (D, 3, D), D ** -0.5, 0.1875, ((0, 32), (2, 8)))
    qk_gain = jnp.clip(1.0 + 0.15 * jax.random.normal(key_of[5], (2, HEADS, HD), jnp.float32), 0.25, 1.75)
    out_weight = normal_values(key_of[6], (D, D), D ** -0.5, 0.1875, ((0, 8), (1, 32)))
    norm2_gain = jnp.clip(1.0 + 0.15 * jax.random.normal(key_of[7], (D,), jnp.float32), 0.25, 1.75)
    up_weight = normal_values(key_of[8], (D, FF), D ** -0.5, 0.1875, ((0, 32), (1, 8)))
    down_weight = normal_values(key_of[9], (FF, D), FF ** -0.5, 0.09375, ((0, 8), (1, 32)))
    return dict(tokens=tokens, win_first=win_first, win_count=win_count, norm1_gain=norm1_gain, qkv_weight=qkv_weight, qk_gain=qk_gain, out_weight=out_weight, norm2_gain=norm2_gain, up_weight=up_weight, down_weight=down_weight)


def layer_norm(rows, gain):
    values = rows.astype(jnp.float32)
    center = values - lax.optimization_barrier(jnp.mean(values, axis=-1, keepdims=True))
    spread = lax.optimization_barrier(jnp.mean(center * center, axis=-1, keepdims=True))
    return (center * lax.rsqrt(spread + 1e-06) * gain).astype(jnp.bfloat16)

def head_norm(values, gain):
    scale = lax.rsqrt(lax.optimization_barrier(jnp.mean(values * values, axis=-1, keepdims=True)) + 1e-06)
    return (values * scale * gain).astype(jnp.bfloat16)

def reference(tokens, win_first, win_count, norm1_gain, qkv_weight, qk_gain, out_weight, norm2_gain, up_weight, down_weight):
    normed_one = layer_norm(tokens, norm1_gain)
    qkv = jnp.dot(normed_one, qkv_weight.reshape(D, 3 * D), preferred_element_type=jnp.float32)
    qkv = qkv.reshape(TOKENS, 3, HEADS, HD)
    queries = head_norm(qkv[:, 0], qk_gain[0])
    keys = head_norm(qkv[:, 1], qk_gain[1])
    values = qkv[:, 2].astype(jnp.bfloat16)
    border = jnp.zeros((WIN_MOST, HEADS, HD), jnp.bfloat16)
    keys_padded = jnp.concatenate([border, keys, border], axis=0)
    values_padded = jnp.concatenate([border, values, border], axis=0)
    row_block = math.gcd(512, TOKENS)
    key_span = row_block + 2 * WIN_MOST
    scale = HD ** (-0.5)

    def attend(index):
        first_row = index * row_block
        query_part = lax.dynamic_slice_in_dim(queries, first_row, row_block, 0).astype(jnp.float32)
        key_part = lax.dynamic_slice_in_dim(keys_padded, first_row, key_span, 0).astype(jnp.float32)
        value_part = lax.dynamic_slice_in_dim(values_padded, first_row, key_span, 0).astype(jnp.float32)
        scores = jnp.einsum('qhd,khd->hqk', query_part, key_part) * scale
        lower = lax.dynamic_slice_in_dim(win_first, first_row, row_block, 0)
        upper = lower + lax.dynamic_slice_in_dim(win_count, first_row, row_block, 0)
        key_index = first_row - WIN_MOST + jnp.arange(key_span, dtype=jnp.int32)
        allowed = (key_index[None, :] >= lower[:, None]) & (key_index[None, :] < upper[:, None])
        weights = jnp.where(allowed[None], jnp.exp(scores), jnp.float32(0.0))
        total = lax.optimization_barrier(jnp.sum(weights, axis=-1, keepdims=True))
        probs = (weights / total).astype(jnp.bfloat16)
        mixed = jnp.einsum('hqk,khd->qhd', probs.astype(jnp.float32), value_part)
        return mixed.astype(jnp.bfloat16).reshape(row_block, D)
    attended = lax.map(attend, jnp.arange(TOKENS // row_block, dtype=jnp.int32)).reshape(TOKENS, D)
    attn_sum = jnp.dot(attended, out_weight, preferred_element_type=jnp.float32)
    middle = (tokens.astype(jnp.float32) + attn_sum).astype(jnp.bfloat16)
    normed_two = layer_norm(middle, norm2_gain)
    hidden = jax.nn.gelu(jnp.dot(normed_two, up_weight, preferred_element_type=jnp.float32), approximate=True).astype(jnp.bfloat16)
    mlp_sum = jnp.dot(hidden, down_weight, preferred_element_type=jnp.float32)
    return (middle.astype(jnp.float32) + mlp_sum).astype(jnp.bfloat16)
```

```python
import jax
import jax.numpy as jnp
from jax import lax
from jax.sharding import Mesh, PartitionSpec as P

WIN_MOST = 64


def layer_norm(rows, gain):
    values = rows.astype(jnp.float32)
    center = values - jnp.mean(values, axis=-1, keepdims=True)
    spread = jnp.mean(center * center, axis=-1, keepdims=True)
    return (center * lax.rsqrt(spread + 1e-06) * gain).astype(jnp.bfloat16)


def head_norm(values, gain):
    scale = lax.rsqrt(jnp.mean(values * values, axis=-1, keepdims=True) + 1e-06)
    return (values * scale * gain).astype(jnp.bfloat16)


def fetch(value, axis, step):
    n = lax.axis_size(axis)
    return lax.ppermute(value, axis, [((i + step) % n, i) for i in range(n)])


def fetch_all(value, axis):
    n = lax.axis_size(axis)
    near = sorted(range(1, n), key=lambda k: -min(k, n - k))
    got = {k: fetch(value, axis, k) for k in near}
    got[0] = value
    return [got[k] for k in range(n)]


def placed(blocks, axis):
    n, rows = len(blocks), blocks[0].shape[0]
    twice = jnp.concatenate(blocks + blocks, axis=0)
    start = (n - lax.axis_index(axis)) * rows
    return lax.dynamic_slice_in_dim(twice, start, n * rows, axis=0)


def gather_zx(value):
    rows, width = value.shape
    along_z = placed([v[None] for v in fetch_all(value, "z")], "z")
    along_x = placed([v[None] for v in fetch_all(along_z, "x")], "x")
    return jnp.swapaxes(along_x, 0, 1).reshape(-1, width)


def local(
    tokens,
    win_first,
    win_count,
    norm1_gain,
    qkv_weight,
    qk_gain,
    out_weight,
    norm2_gain,
    up_weight,
    down_weight,
):
    rows, model = tokens.shape
    n_y = lax.axis_size("y")
    core = lax.axis_index("core")
    y = lax.axis_index("y")
    seq_rows = rows * n_y * 2
    local_heads, head_width = qk_gain.shape[1:]
    columns = local_heads * head_width

    normed_one = layer_norm(tokens, norm1_gain)
    mine = placed([v[None] for v in fetch_all(normed_one, "y")], "y")
    qkv_full = gather_zx(qkv_weight.reshape(-1, 3 * columns))
    out_own = jnp.concatenate(fetch_all(out_weight.T, "y"), axis=1)
    out_own = gather_zx(out_own)
    both = gather_zx(jnp.concatenate([up_weight, down_weight.T], axis=1))
    other = fetch(mine, "core", 1)
    first = core == 0
    piece = jnp.stack(
        [jnp.where(first, mine, other), jnp.where(first, other, mine)], axis=1
    ).reshape(seq_rows, model)

    qkv = jnp.dot(piece, qkv_full, preferred_element_type=jnp.float32).reshape(
        seq_rows, 3, columns
    )
    queries = head_norm(qkv[:, 0].reshape(seq_rows, local_heads, head_width), qk_gain[0])
    keys = head_norm(qkv[:, 1].reshape(seq_rows, local_heads, head_width), qk_gain[1])
    values = qkv[:, 2].astype(jnp.bfloat16)
    stacked = jnp.concatenate([keys.reshape(seq_rows, columns), values], axis=1)
    n_seq = lax.axis_size("z") * lax.axis_size("x")
    up = [(i, i + 1) for i in range(n_seq - 1)]
    down = [(i + 1, i) for i in range(n_seq - 1)]
    before = lax.ppermute(stacked[-WIN_MOST:], ("z", "x"), up)
    after = lax.ppermute(stacked[:WIN_MOST], ("z", "x"), down)
    padded = jnp.concatenate([before, stacked, after], axis=0)
    row_block = 512
    key_span = row_block + 2 * WIN_MOST
    scale = head_width ** (-0.5)
    anchor = (lax.axis_index("z") * lax.axis_size("x") + lax.axis_index("x")) * seq_rows
    outputs = []
    for first_row in range(0, seq_rows, row_block):
        query_part = queries[first_row : first_row + row_block]
        key_block = padded[first_row : first_row + key_span]
        key_part = key_block[:, :columns].reshape(key_span, local_heads, head_width)
        value_part = key_block[:, columns:].reshape(key_span, local_heads, head_width)
        scores = (
            jnp.einsum("qhd,khd->hqk", query_part, key_part, preferred_element_type=jnp.float32)
            * scale
        )
        lower = win_first[first_row : first_row + row_block]
        upper = lower + win_count[first_row : first_row + row_block]
        key_index = anchor + (first_row - WIN_MOST) + jnp.arange(key_span, dtype=jnp.int32)
        allowed = (key_index[None, :] >= lower[:, None]) & (key_index[None, :] < upper[:, None])
        weights = jnp.where(allowed[None], jnp.exp(scores), jnp.float32(0.0))
        total = jnp.sum(weights, axis=-1, keepdims=True)
        probs = (weights / total).astype(jnp.bfloat16)
        mixed = jnp.einsum("hqk,khd->qhd", probs, value_part, preferred_element_type=jnp.float32)
        outputs.append(mixed.astype(jnp.bfloat16).reshape(row_block, columns))
    attended = jnp.concatenate(outputs, axis=0).reshape(n_y, 2, rows, columns)

    keep = jnp.where(first, attended[:, 0], attended[:, 1])
    give = jnp.where(first, attended[:, 1], attended[:, 0])
    got = fetch(give, "core", 1)
    wide = jnp.concatenate([keep, got], axis=-1)
    parts = []
    for k in range(n_y):
        if k == 0:
            parts.append(lax.dynamic_index_in_dim(wide, y, 0, keepdims=False))
        else:
            to = lax.dynamic_index_in_dim(wide, (y - k) % n_y, 0, keepdims=False)
            parts.append(fetch(to, "y", k))
    att_own = jnp.concatenate([p[:, :columns] for p in parts], axis=1)
    att_other = jnp.concatenate([p[:, columns:] for p in parts], axis=1)
    out_other = fetch(out_own, "core", 1)
    contract = (((1,), (1,)), ((), ()))
    attn_sum = lax.dot_general(
        att_own, out_own, contract, preferred_element_type=jnp.float32
    ) + lax.dot_general(att_other, out_other, contract, preferred_element_type=jnp.float32)
    middle = (tokens.astype(jnp.float32) + attn_sum).astype(jnp.bfloat16)

    normed_two = layer_norm(middle, norm2_gain)
    hidden_part = up_weight.shape[1]
    both_other = fetch(both, "core", 1)
    up_full = jnp.concatenate([both[:, :hidden_part], both_other[:, :hidden_part]], axis=1)
    down_full = jnp.concatenate([both[:, hidden_part:], both_other[:, hidden_part:]], axis=1)
    total = middle.astype(jnp.float32)
    blocks = fetch_all(normed_two, "y")
    for k in (0, 3, 2, 1):
        hidden = jax.nn.gelu(
            jnp.dot(blocks[k], up_full, preferred_element_type=jnp.float32), approximate=True
        ).astype(jnp.bfloat16)
        share = lax.dot_general(hidden, down_full, contract, preferred_element_type=jnp.float32)
        if k == 0:
            total = total + share
        else:
            total = total + fetch(share.astype(jnp.bfloat16), "y", n_y - k).astype(jnp.float32)
    return total.astype(jnp.bfloat16)


def solution(mesh):
    devices = mesh.devices.reshape(8, 4, 4, 2)
    fine = Mesh(devices, ("z", "x", "y", "core"))
    seq, head = ("z", "x"), ("y", "core")
    return jax.shard_map(
        local,
        mesh=fine,
        in_specs=(
            P(seq + head, None),
            P(seq),
            P(seq),
            P(),
            P(seq, None, head),
            P(None, head, None),
            P(head, seq),
            P(),
            P(seq, head),
            P(head, seq),
        ),
        out_specs=P(seq + head, None),
        check_vma=False,
    )
```

```python
import functools

import jax
import jax.numpy as jnp
from jax import lax
from jax.experimental import pallas as pl
from jax.experimental.pallas import tpu as pltpu
from jax.sharding import Mesh, PartitionSpec as P

WIN = 64
F32, BF16 = jnp.float32, jnp.bfloat16
NT = (((1,), (1,)), ((), ()))
VMEM = pl.BlockSpec(memory_space=pltpu.VMEM)
SMEM = pl.BlockSpec(memory_space=pltpu.SMEM)


def params(mib):
    return pltpu.CompilerParams(vmem_limit_bytes=mib * 2**20)


def layer_norm(values, gain):
    center = values - jnp.mean(values, axis=-1, keepdims=True)
    spread = jnp.mean(center * center, axis=-1, keepdims=True)
    return (center * lax.rsqrt(spread + 1e-06) * gain).astype(BF16)


def head_norm(values, gain, half):
    square = values * values
    low = jnp.sum(jnp.where(half, square, 0.0), axis=-1, keepdims=True)
    high = jnp.sum(jnp.where(half, 0.0, square), axis=-1, keepdims=True)
    scale = lax.rsqrt(jnp.where(half, low, high) * (1.0 / 64) + 1e-06)
    return (values * scale * gain).astype(BF16)


def first_half(rows):
    return lax.broadcasted_iota(jnp.int32, (rows, 128), 1) < 64


def start_kernel(tok, gain, qkv, out_w, up, down, normed, front, back):
    normed[...] = layer_norm(tok[...].astype(F32), gain[...])
    pack = jnp.concatenate(
        [qkv[:, 0], qkv[:, 1], qkv[:, 2], out_w[...].astype(F32).T.astype(BF16)], axis=1
    )
    for i in range(front.shape[0]):
        front[i] = pack
    back[:, :512] = up[...]
    back[:, 512:] = down[...].astype(F32).T.astype(BF16)


def edge_kernel(at, *refs):
    own, peer = refs[:4], refs[4:8]
    weight, gain, head_kv, tail_kv, rows = refs[8:]
    y, core = at[0], at[1]
    for k in range(4):

        @pl.when(lax.rem(y + k, 4) == 0)
        def _():
            rows[:WIN] = jnp.where(core == 0, own[k][:WIN], peer[k][:WIN])

        @pl.when(lax.rem(y + k, 4) == 3)
        def _():
            rows[WIN:] = jnp.where(core == 1, own[k][128 - WIN :], peer[k][128 - WIN :])

    kv = jnp.dot(rows[...], weight[:, 128:384], preferred_element_type=F32)
    key = head_norm(kv[:, :128], gain[1:2], first_half(128))
    both = jnp.concatenate([key, kv[:, 128:].astype(BF16)], axis=1)
    head_kv[...] = both[:WIN]
    tail_kv[...] = both[WIN:]


def attend(query, kv, first, count, key_start):
    lower = jnp.broadcast_to(first, (128, 128)).T
    upper = lower + jnp.broadcast_to(count, (128, 128)).T
    index = key_start + lax.broadcasted_iota(jnp.int32, (128, 256), 1)
    lower = jnp.concatenate([lower, lower], axis=1)
    upper = jnp.concatenate([upper, upper], axis=1)
    allowed = (index >= lower) & (index < upper)
    outs = []
    for h in range(2):
        lanes = slice(h * 64, h * 64 + 64)
        score = lax.dot_general(query[:, lanes], kv[:, lanes], NT, preferred_element_type=F32)
        weight = jnp.where(allowed, jnp.exp(score * 0.125), 0.0)
        total = jnp.sum(weight, axis=-1, keepdims=True)
        prob = (weight / total).astype(BF16)
        value = kv[:, 128 + h * 64 : 192 + h * 64]
        outs.append(jnp.dot(prob, value, preferred_element_type=F32))
    return jnp.concatenate(outs, axis=1).astype(BF16)


def main_kernel(at, *refs):
    own, peer = refs[:4], refs[4:8]
    weight, gain, first, count, att, q_edge, kv_edge, q_s, kv_s = refs[8:]
    y, core, anchor = at[0], at[1], at[2]
    half = first_half(256)
    for k in range(4):
        rows = jnp.concatenate([own[k][...], peer[k][...]], axis=0)
        qkv = jnp.dot(rows, weight[:, :384], preferred_element_type=F32)
        query = head_norm(qkv[:, :128], gain[0:1], half)
        key = head_norm(qkv[:, 128:256], gain[1:2], half)
        kv = jnp.concatenate([key, qkv[:, 256:].astype(BF16)], axis=1)
        base = lax.rem(y + k, 4) * 256
        mine = pl.multiple_of(base + core * 128, 128)
        theirs = pl.multiple_of(base + (1 - core) * 128, 128)
        q_s[pl.ds(mine, 128)] = query[:128]
        q_s[pl.ds(theirs, 128)] = query[128:]
        kv_s[pl.ds(mine, 128)] = kv[:128]
        kv_s[pl.ds(theirs, 128)] = kv[128:]
    for b in range(1, 7):
        start = b * 128 - WIN
        att[lax.rem(core + b, 2), b // 2] = attend(
            q_s[b * 128 : b * 128 + 128],
            kv_s[start : start + 256],
            first[b : b + 1],
            count[b : b + 1],
            anchor + start,
        )
    zero = jnp.zeros((128, 128), BF16)
    att[core, 0] = zero
    att[lax.rem(core + 1, 2), 3] = zero
    q_edge[0] = q_s[:128]
    q_edge[1] = q_s[896:]
    kv_edge[0] = kv_s[:192]
    kv_edge[1] = kv_s[832:]


def last_kernel(at, att, q_edge, kv_edge, before, after, first, count, out):
    core, anchor = at[1], at[2]
    out[...] = att[...]
    top = jnp.concatenate([before[...], kv_edge[0]], axis=0)
    out[core, 0] = attend(q_edge[0], top, first[0:1], count[0:1], anchor - WIN)
    bottom = jnp.concatenate([kv_edge[1], after[...]], axis=0)
    out[lax.rem(core + 1, 2), 3] = attend(
        q_edge[1], bottom, first[7:8], count[7:8], anchor + 896 - WIN
    )


def project_kernel(at, att, got, weight, other, mine, away):
    y = at[0]
    for k in (2, 1, 3, 0):
        t = lax.rem(y + k, 4)
        part = lax.dot_general(
            att[0, t], weight[:, 384:], NT, preferred_element_type=F32
        ) + lax.dot_general(got[t], other[...], NT, preferred_element_type=F32)
        if k == 0:
            mine[...] = part
        else:
            away[k - 1] = part.astype(BF16)


def middle_kernel(tok, mine, a, b, c, gain, middle, normed):
    total = mine[...] + a[...].astype(F32) + b[...].astype(F32) + c[...].astype(F32)
    mid = (tok[...].astype(F32) + total).astype(BF16)
    middle[...] = mid
    normed[...] = layer_norm(mid.astype(F32), gain[...])


def mlp_kernel(rows, up_own, down_own, up_peer, down_peer, out, total):
    step = pl.program_id(0)
    up = jnp.concatenate([up_own[...], up_peer[...]], axis=1)
    down = jnp.concatenate([down_own[...], down_peer[...]], axis=1)
    hidden = jax.nn.gelu(
        jnp.dot(rows[...], up, preferred_element_type=F32), approximate=True
    ).astype(BF16)
    part = lax.dot_general(hidden, down, NT, preferred_element_type=F32)

    @pl.when(step == 0)
    def _():
        total[...] = part

    @pl.when(step == 1)
    def _():
        out[...] = (total[...] + part).astype(out.dtype)


def mlp(rows, own, peer, dtype):
    block = lambda at: pl.BlockSpec((1024, 256), lambda i, at=at: (0, at + i))
    whole = pl.BlockSpec((128, 1024), lambda i: (0, 0))
    return pl.pallas_call(
        mlp_kernel,
        grid=(2,),
        out_shape=jax.ShapeDtypeStruct((128, 1024), dtype),
        in_specs=[whole, block(0), block(2), block(0), block(2)],
        out_specs=whole,
        scratch_shapes=[pltpu.VMEM((128, 1024), F32)],
        compiler_params=params(24),
        cost_estimate=pl.CostEstimate(flops=4 * 128 * 2**20, bytes_accessed=5 * 2**20, transcendentals=2**17),
        name="mlp",
    )(rows, own, own, peer, peer)


def end_kernel(middle, mine, a, b, c, out):
    total = middle[...].astype(F32) + mine[...]
    total += a[...].astype(F32) + b[...].astype(F32) + c[...].astype(F32)
    out[...] = total.astype(BF16)


def call(kernel, outs, specs, name, mib=24, scratch=(), flops=2**20, **more):
    return pl.pallas_call(
        kernel,
        out_shape=[jax.ShapeDtypeStruct(s, d) for s, d in outs],
        in_specs=specs,
        out_specs=[VMEM] * len(outs),
        scratch_shapes=list(scratch),
        compiler_params=params(mib),
        cost_estimate=pl.CostEstimate(flops=flops, bytes_accessed=2**21, transcendentals=0),
        name=name,
        **more,
    )


def fetch(value, axis, step):
    n = lax.axis_size(axis)
    return lax.ppermute(value, axis, [((i + step) % n, i) for i in range(n)])


def local(
    tokens,
    win_first,
    win_count,
    norm1_gain,
    qkv_weight,
    qk_gain,
    out_weight,
    norm2_gain,
    up_weight,
    down_weight,
):
    y, core = lax.axis_index("y"), lax.axis_index("core")
    seq = lax.axis_index("z") * lax.axis_size("x") + lax.axis_index("x")
    at = jnp.stack([y, core, seq * 1024]).astype(jnp.int32)
    first, count = win_first.reshape(8, 128), win_count.reshape(8, 128)
    gain = qk_gain.reshape(2, 128)

    normed, front, back = call(
        start_kernel,
        [((128, 1024), BF16), ((32, 32, 512), BF16), ((32, 1024), BF16)],
        [VMEM] * 6,
        "start",
    )(tokens, norm1_gain.reshape(1, 1024), qkv_weight, out_weight, up_weight, down_weight)

    mlp_own = lax.all_gather(back, ("z", "x"), axis=0, tiled=True)
    far = {k: fetch(normed, "y", k) for k in (2, 1, 3)}
    own = [normed, far[1], far[2], far[3]]
    peer = [fetch(rows, "core", 1) for rows in own]
    weight = lax.all_to_all(front, ("z", "x"), 0, 0, tiled=True).reshape(1024, 512)
    out_peer = fetch(weight[:, 384:], "core", 1)

    head_kv, tail_kv = call(
        edge_kernel,
        [((WIN, 256), BF16)] * 2,
        [SMEM] + [VMEM] * 10,
        "edge",
        scratch=[pltpu.VMEM((2 * WIN, 1024), BF16)],
    )(at, *own, *peer, weight, gain)
    n_seq = lax.axis_size("z") * lax.axis_size("x")
    before = lax.ppermute(tail_kv, ("z", "x"), [(i, (i + 1) % n_seq) for i in range(n_seq)])
    after = lax.ppermute(head_kv, ("z", "x"), [((i + 1) % n_seq, i) for i in range(n_seq)])
    att, q_edge, kv_edge = call(
        main_kernel,
        [((2, 4, 128, 128), BF16), ((2, 128, 128), BF16), ((2, 192, 256), BF16)],
        [SMEM] + [VMEM] * 12,
        "attention",
        scratch=[pltpu.VMEM((1024, 128), BF16), pltpu.VMEM((1024, 256), BF16)],
        flops=5 * 2**30,
    )(at, *own, *peer, weight, gain, first, count)
    (att,) = call(
        last_kernel,
        [((2, 4, 128, 128), BF16)],
        [SMEM] + [VMEM] * 7,
        "attention_edge",
    )(at, att, q_edge, kv_edge, before, after, first, count)

    got = fetch(att[1], "core", 1)
    mine, away = call(
        project_kernel,
        [((128, 1024), F32), ((3, 128, 1024), BF16)],
        [SMEM] + [VMEM] * 4,
        "project",
    )(at, att, got, weight, out_peer)
    parts = [fetch(away[k - 1], "y", 4 - k) for k in (2, 1, 3)]
    middle, normed_two = call(
        middle_kernel,
        [((128, 1024), BF16)] * 2,
        [VMEM] * 6,
        "middle",
    )(tokens, mine, *parts, norm2_gain.reshape(1, 1024))

    mlp_own, _ = lax.optimization_barrier((mlp_own, normed_two))
    mlp_peer = fetch(mlp_own, "core", 1)
    far = {k: fetch(normed_two, "y", k) for k in (2, 1, 3)}
    mine = mlp(normed_two, mlp_own, mlp_peer, F32)
    parts = [fetch(mlp(far[k], mlp_own, mlp_peer, BF16), "y", 4 - k) for k in (3, 2, 1)]
    (out,) = call(end_kernel, [((128, 1024), BF16)], [VMEM] * 5, "end")(middle, mine, *parts)
    return out


def solution(mesh):
    fine = Mesh(mesh.devices.reshape(8, 4, 4, 2), ("z", "x", "y", "core"))
    seq, head = ("z", "x"), ("y", "core")
    return jax.shard_map(
        local,
        mesh=fine,
        in_specs=(
            P(seq + head, None),
            P(seq),
            P(seq),
            P(),
            P(seq, None, head),
            P(None, head, None),
            P(head, seq),
            P(),
            P(seq, head),
            P(head, seq),
        ),
        out_specs=P(seq + head, None),
        check_vma=False,
    )
```

```python
import functools

import jax
import jax.numpy as jnp
from jax import lax
from jax.experimental import pallas as pl
from jax.experimental.pallas import tpu as pltpu
from jax.sharding import Mesh, PartitionSpec as P

WIN = 64
F32, BF16 = jnp.float32, jnp.bfloat16
NT = (((1,), (1,)), ((), ()))
VMEM = pl.BlockSpec(memory_space=pltpu.VMEM)
SMEM = pl.BlockSpec(memory_space=pltpu.SMEM)


def params(mib):
    return pltpu.CompilerParams(vmem_limit_bytes=mib * 2**20)


def layer_norm(values, gain):
    center = values - jnp.mean(values, axis=-1, keepdims=True)
    spread = jnp.mean(center * center, axis=-1, keepdims=True)
    return (center * lax.rsqrt(spread + 1e-06) * gain).astype(BF16)


def head_norm(values, gain, half):
    square = values * values
    low = jnp.sum(jnp.where(half, square, 0.0), axis=-1, keepdims=True)
    high = jnp.sum(jnp.where(half, 0.0, square), axis=-1, keepdims=True)
    scale = lax.rsqrt(jnp.where(half, low, high) * (1.0 / 64) + 1e-06)
    return (values * scale * gain).astype(BF16)


def first_half(rows):
    return lax.broadcasted_iota(jnp.int32, (rows, 128), 1) < 64


def start_kernel(tok, gain, qkv, out_t, normed, front):
    normed[...] = layer_norm(tok[...].astype(F32), gain[...])
    pack = jnp.concatenate([qkv[0], qkv[1], qkv[2], out_t[...]], axis=1)
    for i in range(8):
        front[i] = pack


def mlp_pack_kernel(up, down_t, back):
    pack = jnp.concatenate([up[...], down_t[...]], axis=1)
    for i in range(8):
        back[i] = pack


def collect_kernel(at, *refs):
    blocks, own, border = refs[:4], refs[4], refs[5]
    y, core = at[0], at[1]
    for k in range(4):
        t = lax.rem(y + k, 4)
        own[t] = blocks[k][...]

        @pl.when((core == 0) & (t == 0))
        def _():
            border[...] = blocks[k][:WIN]

        @pl.when((core == 1) & (t == 3))
        def _():
            border[...] = blocks[k][128 - WIN :]


def lay_kernel(at, *refs):
    blocks, out = refs[:4], refs[4]
    for k in range(4):
        base = lax.rem(at[2] + k, 4) * 32
        for z in range(8):
            out[pl.ds(pl.multiple_of(z * 128 + base, 32), 32)] = blocks[k][z]


def attend(query, kv, first, count, key_start):
    lower = jnp.broadcast_to(first, (128, 128)).T
    upper = lower + jnp.broadcast_to(count, (128, 128)).T
    index = key_start + lax.broadcasted_iota(jnp.int32, (128, 256), 1)
    lower = jnp.concatenate([lower, lower], axis=1)
    upper = jnp.concatenate([upper, upper], axis=1)
    allowed = (index >= lower) & (index < upper)
    outs = []
    for h in range(2):
        lanes = slice(h * 64, h * 64 + 64)
        score = lax.dot_general(query[:, lanes], kv[:, lanes], NT, preferred_element_type=F32)
        weight = jnp.where(allowed, jnp.exp(score * 0.125), 0.0)
        total = jnp.sum(weight, axis=-1, keepdims=True)
        prob = (weight / total).astype(BF16)
        value = kv[:, 128 + h * 64 : 192 + h * 64]
        outs.append(jnp.dot(prob, value, preferred_element_type=F32))
    return jnp.concatenate(outs, axis=1).astype(BF16)


def attention_kernel(at, *refs):
    own, peer, blocks = refs[0], refs[1], refs[2:6]
    near_own, near_peer, gain, first, count, att, weight, q_s, kv_s = refs[6:]
    core, anchor = at[1], at[3]
    for k in range(4):
        base = lax.rem(at[2] + k, 4) * 32
        for z in range(8):
            weight[pl.ds(pl.multiple_of(z * 128 + base, 32), 32)] = blocks[k][z]

    rows = jnp.concatenate([near_own[...], near_peer[...]], axis=0)
    part = jnp.dot(rows, weight[:, 128:], preferred_element_type=F32)
    key = head_norm(part[:, :128], gain[1:2], first_half(2 * WIN))
    kv = jnp.concatenate([key, part[:, 128:].astype(BF16)], axis=1)
    end = WIN + 1024
    kv_s[pl.ds(pl.multiple_of((1 - core) * end, WIN), WIN)] = kv[:WIN]
    kv_s[pl.ds(pl.multiple_of(core * end, WIN), WIN)] = kv[WIN:]

    half = first_half(256)
    for t in range(4):
        rows = jnp.concatenate([own[t], peer[t]], axis=0)
        qkv = jnp.dot(rows, weight[...], preferred_element_type=F32)
        query = head_norm(qkv[:, :128], gain[0:1], half)
        key = head_norm(qkv[:, 128:256], gain[1:2], half)
        kv = jnp.concatenate([key, qkv[:, 256:].astype(BF16)], axis=1)
        mine = pl.multiple_of(t * 256 + core * 128, 128)
        theirs = pl.multiple_of(t * 256 + (1 - core) * 128, 128)
        q_s[pl.ds(mine, 128)] = query[:128]
        q_s[pl.ds(theirs, 128)] = query[128:]
        kv_s[pl.ds(pl.multiple_of(mine + WIN, WIN), 128)] = kv[:128]
        kv_s[pl.ds(pl.multiple_of(theirs + WIN, WIN), 128)] = kv[128:]
    for b in range(8):
        att[lax.rem(core + b, 2), b // 2] = attend(
            q_s[b * 128 : b * 128 + 128],
            kv_s[b * 128 : b * 128 + 256],
            first[b : b + 1],
            count[b : b + 1],
            anchor + (b * 128 - WIN),
        )


def project_kernel(at, att, got, weight, other, mine, away):
    y = at[0]
    for k in (2, 1, 3, 0):
        t = lax.rem(y + k, 4)
        part = lax.dot_general(
            att[0, t], weight[...], NT, preferred_element_type=F32
        ) + lax.dot_general(got[t], other[...], NT, preferred_element_type=F32)
        if k == 0:
            mine[...] = part
        else:
            away[k - 1] = part.astype(BF16)


def middle_kernel(tok, mine, a, b, c, gain, middle, normed):
    total = mine[...] + a[...].astype(F32) + b[...].astype(F32) + c[...].astype(F32)
    mid = (tok[...].astype(F32) + total).astype(BF16)
    middle[...] = mid
    normed[...] = layer_norm(mid.astype(F32), gain[...])


def mlp_kernel(rows, up_own, down_own, up_peer, down_peer, out, total):
    step = pl.program_id(0)
    up = jnp.concatenate([up_own[...], up_peer[...]], axis=1)
    down = jnp.concatenate([down_own[...], down_peer[...]], axis=1)
    hidden = jax.nn.gelu(
        jnp.dot(rows[...], up, preferred_element_type=F32), approximate=True
    ).astype(BF16)
    part = lax.dot_general(hidden, down, NT, preferred_element_type=F32)

    @pl.when(step == 0)
    def _():
        total[...] = part

    @pl.when(step == 1)
    def _():
        out[...] = (total[...] + part).astype(out.dtype)


def mlp(rows, own, peer, dtype):
    block = lambda at: pl.BlockSpec((1024, 256), lambda i, at=at: (0, at + i))
    whole = pl.BlockSpec((128, 1024), lambda i: (0, 0))
    return pl.pallas_call(
        mlp_kernel,
        grid=(2,),
        out_shape=jax.ShapeDtypeStruct((128, 1024), dtype),
        in_specs=[whole, block(0), block(2), block(0), block(2)],
        out_specs=whole,
        scratch_shapes=[pltpu.VMEM((128, 1024), F32)],
        compiler_params=params(8),
        cost_estimate=pl.CostEstimate(flops=4 * 128 * 2**20, bytes_accessed=5 * 2**20, transcendentals=2**17),
        name="mlp",
    )(rows, own, own, peer, peer)


def end_kernel(middle, mine, a, b, c, out):
    total = middle[...].astype(F32) + mine[...]
    total += a[...].astype(F32) + b[...].astype(F32) + c[...].astype(F32)
    out[...] = total.astype(BF16)


def call(kernel, outs, specs, name, mib=8, scratch=(), flops=2**20, **more):
    return pl.pallas_call(
        kernel,
        out_shape=[jax.ShapeDtypeStruct(s, d) for s, d in outs],
        in_specs=specs,
        out_specs=[VMEM] * len(outs),
        scratch_shapes=list(scratch),
        compiler_params=params(mib),
        cost_estimate=pl.CostEstimate(flops=flops, bytes_accessed=2**21, transcendentals=0),
        name=name,
        **more,
    )


def fetch(value, axis, step):
    n = lax.axis_size(axis)
    return lax.ppermute(value, axis, [((i + step) % n, i) for i in range(n)])


def local(
    tokens,
    win_first,
    win_count,
    norm1_gain,
    qkv_weight,
    qk_gain,
    out_weight,
    norm2_gain,
    up_weight,
    down_weight,
):
    y, core = lax.axis_index("y"), lax.axis_index("core")
    seq = lax.axis_index("z") * lax.axis_size("x") + lax.axis_index("x")
    at = jnp.stack([y, core, lax.axis_index("x"), seq * 1024]).astype(jnp.int32)
    first, count = win_first.reshape(8, 128), win_count.reshape(8, 128)
    gain = qk_gain.reshape(2, 128)

    normed, front = call(
        start_kernel,
        [((128, 1024), BF16), ((8, 32, 512), BF16)],
        [VMEM] * 4,
        "start",
    )(
        tokens,
        norm1_gain.reshape(1, 1024),
        jnp.transpose(qkv_weight, (1, 0, 2)),
        out_weight.T,
    )
    (back,) = call(mlp_pack_kernel, [((8, 32, 1024), BF16)], [VMEM] * 2, "mlp_pack")(
        up_weight, down_weight.T
    )
    front = lax.all_to_all(front, "z", 0, 0, tiled=True)
    front, out_block = front[:, :, :384], front[:, :, 384:]
    far = {k: fetch(normed, "y", k) for k in (2, 1, 3)}
    blocks = [front] + [fetch(front, "x", k) for k in (1, 2, 3)]
    back, _ = lax.optimization_barrier((back, front))
    back = lax.all_to_all(back, "z", 0, 0, tiled=True)
    far, _ = lax.optimization_barrier((far, (blocks[1], blocks[3])))
    own, border = call(
        collect_kernel,
        [((4, 128, 1024), BF16), ((WIN, 1024), BF16)],
        [SMEM] + [VMEM] * 4,
        "collect",
    )(at, normed, far[1], far[2], far[3])
    peer = fetch(own, "core", 1)
    out_block, _ = lax.optimization_barrier((out_block, blocks))
    out_blocks = [out_block] + [fetch(out_block, "x", k) for k in (1, 2, 3)]
    spot = lambda z, x, y, core: ((z * 4 + x) * 4 + y) * 2 + core
    shift = lambda s, by: divmod((s + by) % 32, 4)
    near_own = lax.ppermute(
        border,
        ("z", "x", "y", "core"),
        [
            (spot(*divmod(s, 4), j, c), spot(*shift(s, 2 * c - 1), j, c))
            for s in range(32)
            for j in range(4)
            for c in range(2)
        ],
    )
    near_peer = fetch(near_own, "core", 1)
    (att,) = call(
        attention_kernel,
        [((2, 4, 128, 128), BF16)],
        [SMEM] + [VMEM] * 11,
        "attention",
        scratch=[
            pltpu.VMEM((1024, 384), BF16),
            pltpu.VMEM((1024, 128), BF16),
            pltpu.VMEM((1024 + 2 * WIN, 256), BF16),
        ],
        flops=5 * 2**30,
    )(at, own, peer, *blocks, near_own, near_peer, gain, first, count)

    mlp_block, _ = lax.optimization_barrier((back, (att, out_blocks)))
    mlp_blocks = [mlp_block] + [fetch(mlp_block, "x", k) for k in (1, 2, 3)]

    def laid(blocks, width, after, name):
        blocks, _ = lax.optimization_barrier((blocks, after))
        (out,) = call(lay_kernel, [((1024, width), BF16)], [SMEM] + [VMEM] * 4, name)(at, *blocks)
        return out

    weight = laid(out_blocks, 128, att, "out_lay")
    out_peer = fetch(weight, "core", 1)
    got = fetch(att[1], "core", 1)
    mine_attended, away = call(
        project_kernel,
        [((128, 1024), F32), ((3, 128, 1024), BF16)],
        [SMEM] + [VMEM] * 4,
        "project",
    )(at, att, got, weight, out_peer)
    parts = [fetch(away[k - 1], "y", 4 - k) for k in (2, 1, 3)]
    middle, normed_two = call(
        middle_kernel,
        [((128, 1024), BF16)] * 2,
        [VMEM] * 6,
        "middle",
    )(tokens, mine_attended, *parts, norm2_gain.reshape(1, 1024))

    far = {k: fetch(normed_two, "y", k) for k in (2, 1, 3)}
    mlp_own = laid(mlp_blocks, 1024, far, "mlp_lay")
    mlp_peer = fetch(mlp_own, "core", 1)
    mine = mlp(normed_two, mlp_own, mlp_peer, F32)
    parts = [fetch(mlp(far[k], mlp_own, mlp_peer, BF16), "y", 4 - k) for k in (3, 2, 1)]
    (out,) = call(end_kernel, [((128, 1024), BF16)], [VMEM] * 5, "end")(middle, mine, *parts)
    return out


def solution(mesh):
    fine = Mesh(mesh.devices.reshape(8, 4, 4, 2), ("z", "x", "y", "core"))
    seq, head = ("z", "x"), ("y", "core")
    return jax.shard_map(
        local,
        mesh=fine,
        in_specs=(
            P(seq + head, None),
            P(seq),
            P(seq),
            P(),
            P(seq, None, head),
            P(None, head, None),
            P(head, seq),
            P(),
            P(seq, head),
            P(head, seq),
        ),
        out_specs=P(seq + head, None),
        check_vma=False,
    )
```

```python
import functools

import jax
import jax.numpy as jnp
from jax import lax
from jax.experimental import pallas as pl
from jax.experimental.pallas import tpu as pltpu
from jax.sharding import Mesh, PartitionSpec as P

WIN = 64
F32, BF16 = jnp.float32, jnp.bfloat16
NT = (((1,), (1,)), ((), ()))
VMEM = pl.BlockSpec(memory_space=pltpu.VMEM)
HBM = pl.BlockSpec(memory_space=pltpu.HBM)
SMEM = pl.BlockSpec(memory_space=pltpu.SMEM)


def params(mib):
    return pltpu.CompilerParams(vmem_limit_bytes=mib * 2**20)


def layer_norm(values, gain):
    center = values - jnp.mean(values, axis=-1, keepdims=True)
    spread = jnp.mean(center * center, axis=-1, keepdims=True)
    return (center * lax.rsqrt(spread + 1e-06) * gain).astype(BF16)


def head_norm(values, gain, half):
    square = values * values
    low = jnp.sum(jnp.where(half, square, 0.0), axis=-1, keepdims=True)
    high = jnp.sum(jnp.where(half, 0.0, square), axis=-1, keepdims=True)
    scale = lax.rsqrt(jnp.where(half, low, high) * (1.0 / 64) + 1e-06)
    return (values * scale * gain).astype(BF16)


def first_half(rows):
    return lax.broadcasted_iota(jnp.int32, (rows, 128), 1) < 64


def start_kernel(*refs):
    held, (normed, front, back), here, sems = refs[:6], refs[6:9], refs[9:15], refs[15]
    copies = [
        pltpu.make_async_copy(a, b, sems.at[i]) for i, (a, b) in enumerate(zip(held, here))
    ]
    for copy in copies:
        copy.start()
    qkv, out_t, tok, gain, up, down_t = here
    copies[0].wait()
    copies[1].wait()
    pack = jnp.concatenate([qkv[0], qkv[1], qkv[2], out_t[...]], axis=1)
    for i in range(8):
        front[i] = pack
    copies[2].wait()
    copies[3].wait()
    normed[...] = layer_norm(tok[...].astype(F32), gain[...])
    copies[4].wait()
    copies[5].wait()
    pack = jnp.concatenate([up[...], down_t[...]], axis=1)
    for i in range(8):
        back[i] = pack


def collect_kernel(at, *refs):
    blocks, own, border = refs[:4], refs[4], refs[5]
    y, core = at[0], at[1]
    for k in range(4):
        t = lax.rem(y + k, 4)
        own[t] = blocks[k][...]

        @pl.when((core == 0) & (t == 0))
        def _():
            border[...] = blocks[k][:WIN]

        @pl.when((core == 1) & (t == 3))
        def _():
            border[...] = blocks[k][128 - WIN :]


def lay_kernel(at, here, right, up_far, down_far, left, out):
    for k, block in enumerate((here, right, None, left)):
        base = lax.rem(at[2] + k, 4) * 32
        for z in range(8):
            rows = pl.ds(pl.multiple_of(z * 128 + base, 32), 32)
            if block is None:
                out[rows, :512] = up_far[z]
                out[rows, 512:] = down_far[z]
            else:
                out[rows] = block[z]


def attend(query, kv, first, count, key_start):
    lower = jnp.broadcast_to(first, (128, 128)).T
    upper = lower + jnp.broadcast_to(count, (128, 128)).T
    index = key_start + lax.broadcasted_iota(jnp.int32, (128, 256), 1)
    lower = jnp.concatenate([lower, lower], axis=1)
    upper = jnp.concatenate([upper, upper], axis=1)
    allowed = (index >= lower) & (index < upper)
    outs = []
    for h in range(2):
        lanes = slice(h * 64, h * 64 + 64)
        score = lax.dot_general(query[:, lanes], kv[:, lanes], NT, preferred_element_type=F32)
        weight = jnp.where(allowed, jnp.exp(score * 0.125), 0.0)
        total = jnp.sum(weight, axis=-1, keepdims=True)
        prob = (weight / total).astype(BF16)
        value = kv[:, 128 + h * 64 : 192 + h * 64]
        outs.append(jnp.dot(prob, value, preferred_element_type=F32))
    return jnp.concatenate(outs, axis=1).astype(BF16)


def attention_kernel(at, *refs):
    own, peer, blocks = refs[0], refs[1], refs[2:6]
    near_own, near_peer, gain, first, count, att, out_w, weight, q_s, kv_s = refs[6:]
    core, anchor = at[1], at[3]
    for k in range(4):
        base = lax.rem(at[2] + k, 4) * 32
        for z in range(8):
            rows = pl.ds(pl.multiple_of(z * 128 + base, 32), 32)
            weight[rows] = blocks[k][z, :, :384]
            out_w[rows] = blocks[k][z, :, 384:]

    rows = jnp.concatenate([near_own[...], near_peer[...]], axis=0)
    part = jnp.dot(rows, weight[:, 128:], preferred_element_type=F32)
    key = head_norm(part[:, :128], gain[1:2], first_half(2 * WIN))
    kv = jnp.concatenate([key, part[:, 128:].astype(BF16)], axis=1)
    end = WIN + 1024
    kv_s[pl.ds(pl.multiple_of((1 - core) * end, WIN), WIN)] = kv[:WIN]
    kv_s[pl.ds(pl.multiple_of(core * end, WIN), WIN)] = kv[WIN:]

    half = first_half(256)
    for t in range(4):
        rows = jnp.concatenate([own[t], peer[t]], axis=0)
        qkv = jnp.dot(rows, weight[...], preferred_element_type=F32)
        query = head_norm(qkv[:, :128], gain[0:1], half)
        key = head_norm(qkv[:, 128:256], gain[1:2], half)
        kv = jnp.concatenate([key, qkv[:, 256:].astype(BF16)], axis=1)
        mine = pl.multiple_of(t * 256 + core * 128, 128)
        theirs = pl.multiple_of(t * 256 + (1 - core) * 128, 128)
        q_s[pl.ds(mine, 128)] = query[:128]
        q_s[pl.ds(theirs, 128)] = query[128:]
        kv_s[pl.ds(pl.multiple_of(mine + WIN, WIN), 128)] = kv[:128]
        kv_s[pl.ds(pl.multiple_of(theirs + WIN, WIN), 128)] = kv[128:]
    for b in range(8):
        att[lax.rem(core + b, 2), b // 2] = attend(
            q_s[b * 128 : b * 128 + 128],
            kv_s[b * 128 : b * 128 + 256],
            first[b : b + 1],
            count[b : b + 1],
            anchor + (b * 128 - WIN),
        )


def project_kernel(at, att, got, weight, other, mine, away):
    y = at[0]
    for k in (2, 1, 3, 0):
        t = lax.rem(y + k, 4)
        part = lax.dot_general(
            att[0, t], weight[...], NT, preferred_element_type=F32
        ) + lax.dot_general(got[t], other[...], NT, preferred_element_type=F32)
        if k == 0:
            mine[...] = part
        else:
            away[k - 1] = part.astype(BF16)


def middle_kernel(tok, mine, a, b, c, gain, middle, normed):
    total = mine[...] + a[...].astype(F32) + b[...].astype(F32) + c[...].astype(F32)
    mid = (tok[...].astype(F32) + total).astype(BF16)
    middle[...] = mid
    normed[...] = layer_norm(mid.astype(F32), gain[...])


def hidden_share(rows, weight):
    hidden = jax.nn.gelu(
        jnp.dot(rows, weight[:, :512], preferred_element_type=F32), approximate=True
    ).astype(BF16)
    return lax.dot_general(hidden, weight[:, 512:], NT, preferred_element_type=F32)


def mlp_first_kernel(a, b, c, d, weight, out):
    rows = jnp.concatenate([a[...], b[...], c[...], d[...]], axis=0)
    out[...] = hidden_share(rows, weight)


def mlp_second_kernel(rows, weight, part, out, *, at):
    total = part[at * 128 : at * 128 + 128] + hidden_share(rows[...], weight)
    out[...] = total.astype(out.dtype)


def mlp_second(rows, weight, part, at):
    return call(
        functools.partial(mlp_second_kernel, at=at),
        [((128, 1024), F32 if at == 0 else BF16)],
        [VMEM] * 3,
        "mlp_second",
    )(rows, weight, part)[0]


def end_kernel(middle, mine, a, b, c, out):
    total = middle[...].astype(F32) + mine[...]
    total += a[...].astype(F32) + b[...].astype(F32) + c[...].astype(F32)
    out[...] = total.astype(BF16)


def call(kernel, outs, specs, name, mib=8, scratch=(), flops=2**20, **more):
    return pl.pallas_call(
        kernel,
        out_shape=[jax.ShapeDtypeStruct(s, d) for s, d in outs],
        in_specs=specs,
        out_specs=[VMEM] * len(outs),
        scratch_shapes=list(scratch),
        compiler_params=params(mib),
        cost_estimate=pl.CostEstimate(flops=flops, bytes_accessed=2**21, transcendentals=0),
        name=name,
        **more,
    )


def fetch(value, axis, step):
    n = lax.axis_size(axis)
    return lax.ppermute(value, axis, [((i + step) % n, i) for i in range(n)])


def local(
    tokens,
    win_first,
    win_count,
    norm1_gain,
    qkv_weight,
    qk_gain,
    out_weight,
    norm2_gain,
    up_weight,
    down_weight,
):
    y, core = lax.axis_index("y"), lax.axis_index("core")
    seq = lax.axis_index("z") * lax.axis_size("x") + lax.axis_index("x")
    at = jnp.stack([y, core, lax.axis_index("x"), seq * 1024]).astype(jnp.int32)
    first, count = win_first.reshape(8, 128), win_count.reshape(8, 128)
    gain = qk_gain.reshape(2, 128)

    given = [
        jnp.transpose(qkv_weight, (1, 0, 2)),
        out_weight.T,
        tokens,
        norm1_gain.reshape(1, 1024),
        up_weight,
        down_weight.T,
    ]
    normed, front, back = call(
        start_kernel,
        [((128, 1024), BF16), ((8, 32, 512), BF16), ((8, 32, 1024), BF16)],
        [HBM] * 6,
        "start",
        scratch=[pltpu.VMEM(v.shape, v.dtype) for v in given]
        + [pltpu.SemaphoreType.DMA((6,))],
    )(*[pltpu.with_memory_space_constraint(v, pltpu.HBM) for v in given])
    front = lax.all_to_all(front, "z", 0, 0, tiled=True)
    far = {k: fetch(normed, "y", k) for k in (2, 1, 3)}
    blocks = [front] + [fetch(front, "x", k) for k in (1, 2, 3)]
    back, _ = lax.optimization_barrier((back, front))
    back = lax.all_to_all(back, "z", 0, 0, tiled=True)
    far, _ = lax.optimization_barrier((far, (blocks[1], blocks[3])))
    own, border = call(
        collect_kernel,
        [((4, 128, 1024), BF16), ((WIN, 1024), BF16)],
        [SMEM] + [VMEM] * 4,
        "collect",
    )(at, normed, far[1], far[2], far[3])
    peer = fetch(own, "core", 1)
    spot = lambda z, x, y, core: ((z * 4 + x) * 4 + y) * 2 + core
    shift = lambda s, by: divmod((s + by) % 32, 4)
    near_own = lax.ppermute(
        border,
        ("z", "x", "y", "core"),
        [
            (spot(*divmod(s, 4), j, c), spot(*shift(s, 2 * c - 1), j, c))
            for s in range(32)
            for j in range(4)
            for c in range(2)
        ],
    )
    near_peer = fetch(near_own, "core", 1)
    own, back = lax.optimization_barrier((own, back))
    att, weight = call(
        attention_kernel,
        [((2, 4, 128, 128), BF16), ((1024, 128), BF16)],
        [SMEM] + [VMEM] * 11,
        "attention",
        scratch=[
            pltpu.VMEM((1024, 384), BF16),
            pltpu.VMEM((1024, 128), BF16),
            pltpu.VMEM((1024 + 2 * WIN, 256), BF16),
        ],
    )(at, own, peer, *blocks, near_own, near_peer, gain, first, count)

    right, left = fetch(back, "x", 1), fetch(back, "x", 3)
    up_far = fetch(right[:, :, :512], "x", 1)
    down_far = fetch(left[:, :, 512:], "x", 3)

    out_peer = fetch(weight, "core", 1)
    got = fetch(att[1], "core", 1)
    mine_attended, away = call(
        project_kernel,
        [((128, 1024), F32), ((3, 128, 1024), BF16)],
        [SMEM] + [VMEM] * 4,
        "project",
    )(at, att, got, weight, out_peer)
    parts = [fetch(away[k - 1], "y", 4 - k) for k in (2, 1, 3)]
    middle, normed_two = call(
        middle_kernel,
        [((128, 1024), BF16)] * 2,
        [VMEM] * 6,
        "middle",
    )(tokens, mine_attended, *parts, norm2_gain.reshape(1, 1024))

    far = {k: fetch(normed_two, "y", k) for k in (2, 1, 3)}
    laid, far = lax.optimization_barrier(((back, right, up_far, down_far, left), far))
    (mlp_own,) = call(lay_kernel, [((1024, 1024), BF16)], [SMEM] + [VMEM] * 5, "mlp_lay")(
        at, *laid
    )
    mlp_peer = fetch(mlp_own, "core", 1)
    (part,) = call(mlp_first_kernel, [((512, 1024), F32)], [VMEM] * 5, "mlp_first", mib=16)(
        normed_two, far[1], far[2], far[3], mlp_own
    )
    parts = [fetch(mlp_second(far[k], mlp_peer, part, k), "y", 4 - k) for k in (2, 1, 3)]
    mine = mlp_second(normed_two, mlp_peer, part, 0)
    (out,) = call(end_kernel, [((128, 1024), BF16)], [VMEM] * 5, "end")(middle, mine, *parts)
    return out


def solution(mesh):
    fine = Mesh(mesh.devices.reshape(8, 4, 4, 2), ("z", "x", "y", "core"))
    seq, head = ("z", "x"), ("y", "core")
    return jax.shard_map(
        local,
        mesh=fine,
        in_specs=(
            P(seq + head, None),
            P(seq),
            P(seq),
            P(),
            P(seq, None, head),
            P(None, head, None),
            P(head, seq),
            P(),
            P(seq, head),
            P(head, seq),
        ),
        out_specs=P(seq + head, None),
        check_vma=False,
    )
```

```python
import functools

import jax
import jax.numpy as jnp
from jax import lax
from jax.experimental import pallas as pl
from jax.experimental.pallas import tpu as pltpu
from jax.sharding import Mesh, PartitionSpec as P

WIN = 64
F32, BF16 = jnp.float32, jnp.bfloat16
NT = (((1,), (1,)), ((), ()))
VMEM = pl.BlockSpec(memory_space=pltpu.VMEM)
HBM = pl.BlockSpec(memory_space=pltpu.HBM)
SMEM = pl.BlockSpec(memory_space=pltpu.SMEM)


def params(mib):
    return pltpu.CompilerParams(vmem_limit_bytes=mib * 2**20)


def layer_norm(values, gain):
    center = values - jnp.mean(values, axis=-1, keepdims=True)
    spread = jnp.mean(center * center, axis=-1, keepdims=True)
    return (center * lax.rsqrt(spread + 1e-06) * gain).astype(BF16)


def head_norm(values, gain, half):
    square = values * values
    low = jnp.sum(jnp.where(half, square, 0.0), axis=-1, keepdims=True)
    high = jnp.sum(jnp.where(half, 0.0, square), axis=-1, keepdims=True)
    scale = lax.rsqrt(jnp.where(half, low, high) * (1.0 / 64) + 1e-06)
    return (values * scale * gain).astype(BF16)


def first_half(rows):
    return lax.broadcasted_iota(jnp.int32, (rows, 128), 1) < 64


def start_kernel(*refs):
    held, (normed, front, back), here, sems = refs[:6], refs[6:9], refs[9:15], refs[15]
    copies = [
        pltpu.make_async_copy(a, b, sems.at[i]) for i, (a, b) in enumerate(zip(held, here))
    ]
    for copy in copies:
        copy.start()
    qkv, out_t, tok, gain, up, down_t = here
    copies[0].wait()
    copies[1].wait()
    pack = jnp.concatenate([qkv[0], qkv[1], qkv[2], out_t[...]], axis=1)
    for i in range(32):
        front[i] = pack
    copies[2].wait()
    copies[3].wait()
    normed[...] = layer_norm(tok[...].astype(F32), gain[...])
    copies[4].wait()
    copies[5].wait()
    pack = jnp.concatenate([up[...], down_t[...]], axis=1)
    for i in range(8):
        back[i] = pack


def collect_kernel(at, *refs):
    blocks, own, border = refs[:4], refs[4], refs[5]
    y, core = at[0], at[1]
    for k in range(4):
        t = lax.rem(y + k, 4)
        own[t] = blocks[k][...]

        @pl.when((core == 0) & (t == 0))
        def _():
            border[...] = blocks[k][:WIN]

        @pl.when((core == 1) & (t == 3))
        def _():
            border[...] = blocks[k][128 - WIN :]


def lay_kernel(at, here, right, up_far, down_far, left, out):
    for k, block in enumerate((here, right, None, left)):
        base = lax.rem(at[2] + k, 4) * 32
        for z in range(8):
            rows = pl.ds(pl.multiple_of(z * 128 + base, 32), 32)
            if block is None:
                out[rows, :512] = up_far[z]
                out[rows, 512:] = down_far[z]
            else:
                out[rows] = block[z]


def attend(query, kv, first, count, key_start):
    lower = jnp.broadcast_to(first, (128, 128)).T
    upper = lower + jnp.broadcast_to(count, (128, 128)).T
    index = key_start + lax.broadcasted_iota(jnp.int32, (128, 256), 1)
    lower = jnp.concatenate([lower, lower], axis=1)
    upper = jnp.concatenate([upper, upper], axis=1)
    allowed = (index >= lower) & (index < upper)
    outs = []
    for h in range(2):
        lanes = slice(h * 64, h * 64 + 64)
        score = lax.dot_general(query[:, lanes], kv[:, lanes], NT, preferred_element_type=F32)
        weight = jnp.where(allowed, jnp.exp(score * 0.125), 0.0)
        total = jnp.sum(weight, axis=-1, keepdims=True)
        prob = (weight / total).astype(BF16)
        value = kv[:, 128 + h * 64 : 192 + h * 64]
        outs.append(jnp.dot(prob, value, preferred_element_type=F32))
    return jnp.concatenate(outs, axis=1).astype(BF16)


def attention_kernel(
    at, own, peer, weight, near_own, near_peer, gains, first, count,
    keep, give, out_w, q_s, kv_s, att,
):
    core, anchor = at[1], at[3]
    gain = gains[...]
    gain = jnp.concatenate([gain[:, 0], gain[:, 1]], axis=1)
    out_w[...] = weight[:, 384:]

    rows = jnp.concatenate([near_own[...], near_peer[...]], axis=0)
    part = jnp.dot(rows, weight[:, 128:384], preferred_element_type=F32)
    key = head_norm(part[:, :128], gain[1:2], first_half(2 * WIN))
    kv = jnp.concatenate([key, part[:, 128:].astype(BF16)], axis=1)
    end = WIN + 1024
    kv_s[pl.ds(pl.multiple_of((1 - core) * end, WIN), WIN)] = kv[:WIN]
    kv_s[pl.ds(pl.multiple_of(core * end, WIN), WIN)] = kv[WIN:]

    half = first_half(256)
    for t in range(4):
        rows = jnp.concatenate([own[t], peer[t]], axis=0)
        qkv = jnp.dot(rows, weight[:, :384], preferred_element_type=F32)
        query = head_norm(qkv[:, :128], gain[0:1], half)
        key = head_norm(qkv[:, 128:256], gain[1:2], half)
        kv = jnp.concatenate([key, qkv[:, 256:].astype(BF16)], axis=1)
        mine = pl.multiple_of(t * 256 + core * 128, 128)
        theirs = pl.multiple_of(t * 256 + (1 - core) * 128, 128)
        q_s[pl.ds(mine, 128)] = query[:128]
        q_s[pl.ds(theirs, 128)] = query[128:]
        kv_s[pl.ds(pl.multiple_of(mine + WIN, WIN), 128)] = kv[:128]
        kv_s[pl.ds(pl.multiple_of(theirs + WIN, WIN), 128)] = kv[128:]
    for b in range(8):
        att[lax.rem(core + b, 2), b // 2] = attend(
            q_s[b * 128 : b * 128 + 128],
            kv_s[b * 128 : b * 128 + 256],
            first[b : b + 1],
            count[b : b + 1],
            anchor + (b * 128 - WIN),
        )
    keep[...] = att[0]
    give[...] = att[1]


def project_kernel(at, keep, got, weight, other, mine, away):
    y = at[0]
    rows = jnp.concatenate(
        [keep[...].reshape(512, 128), got[...].reshape(512, 128)], axis=1
    )
    both = jnp.concatenate([weight[...], other[...]], axis=1)
    part = lax.dot_general(rows, both, NT, preferred_element_type=F32)
    for t in range(4):
        block = part[t * 128 : t * 128 + 128]

        @pl.when(y == t)
        def _():
            mine[...] = block

        @pl.when(y != t)
        def _():
            away[lax.rem(t + 3 - y, 4)] = block.astype(BF16)


def middle_kernel(tok, mine, a, b, c, gain, middle, normed):
    total = mine[...] + a[...].astype(F32) + b[...].astype(F32) + c[...].astype(F32)
    mid = (tok[...].astype(F32) + total).astype(BF16)
    middle[...] = mid
    normed[...] = layer_norm(mid.astype(F32), gain[...])


def hidden_share(rows, weight):
    hidden = jax.nn.gelu(
        jnp.dot(rows, weight[:, :512], preferred_element_type=F32), approximate=True
    ).astype(BF16)
    return lax.dot_general(hidden, weight[:, 512:], NT, preferred_element_type=F32)


def mlp_first_kernel(a, b, c, d, weight, out):
    rows = jnp.concatenate([a[...], b[...], c[...], d[...]], axis=0)
    out[...] = hidden_share(rows, weight)


def mlp_second_kernel(rows, weight, part, out, *, at):
    total = part[at * 128 : at * 128 + 128] + hidden_share(rows[...], weight)
    out[...] = total.astype(out.dtype)


def mlp_second(rows, weight, part, at):
    return call(
        functools.partial(mlp_second_kernel, at=at),
        [((128, 1024), F32 if at == 0 else BF16)],
        [VMEM] * 3,
        "mlp_second",
    )(rows, weight, part)[0]


def end_kernel(middle, mine, a, b, c, out):
    total = middle[...].astype(F32) + mine[...]
    total += a[...].astype(F32) + b[...].astype(F32) + c[...].astype(F32)
    out[...] = total.astype(BF16)


def call(kernel, outs, specs, name, mib=8, scratch=(), flops=2**20, **more):
    return pl.pallas_call(
        kernel,
        out_shape=[jax.ShapeDtypeStruct(s, d) for s, d in outs],
        in_specs=specs,
        out_specs=[VMEM] * len(outs),
        scratch_shapes=list(scratch),
        compiler_params=params(mib),
        cost_estimate=pl.CostEstimate(flops=flops, bytes_accessed=2**21, transcendentals=0),
        name=name,
        **more,
    )


def fetch(value, axis, step):
    n = lax.axis_size(axis)
    return lax.ppermute(value, axis, [((i + step) % n, i) for i in range(n)])


def local(
    tokens,
    win_first,
    win_count,
    norm1_gain,
    qkv_weight,
    qk_gain,
    out_weight,
    norm2_gain,
    up_weight,
    down_weight,
):
    y, core = lax.axis_index("y"), lax.axis_index("core")
    seq = lax.axis_index("z") * lax.axis_size("x") + lax.axis_index("x")
    at = jnp.stack([y, core, lax.axis_index("x"), seq * 1024]).astype(jnp.int32)
    first, count = win_first.reshape(8, 128), win_count.reshape(8, 128)

    given = [
        jnp.transpose(qkv_weight, (1, 0, 2)),
        out_weight.T,
        tokens,
        norm1_gain.reshape(1, 1024),
        up_weight,
        down_weight.T,
    ]
    normed, front, back = call(
        start_kernel,
        [((128, 1024), BF16), ((32, 32, 512), BF16), ((8, 32, 1024), BF16)],
        [HBM] * 6,
        "start",
        scratch=[pltpu.VMEM(v.shape, v.dtype) for v in given]
        + [pltpu.SemaphoreType.DMA((6,))],
    )(*[pltpu.with_memory_space_constraint(v, pltpu.HBM) for v in given])
    weight = lax.all_to_all(front, ("z", "x"), 0, 0, tiled=True).reshape(1024, 512)
    far = {k: fetch(normed, "y", k) for k in (2, 1, 3)}
    own, border = call(
        collect_kernel,
        [((4, 128, 1024), BF16), ((WIN, 1024), BF16)],
        [SMEM] + [VMEM] * 4,
        "collect",
    )(at, normed, far[1], far[2], far[3])
    peer = fetch(own, "core", 1)
    spot = lambda z, x, y, core: ((z * 4 + x) * 4 + y) * 2 + core
    shift = lambda s, by: divmod((s + by) % 32, 4)
    near_own = lax.ppermute(
        border,
        ("z", "x", "y", "core"),
        [
            (spot(*divmod(s, 4), j, c), spot(*shift(s, 2 * c - 1), j, c))
            for s in range(32)
            for j in range(4)
            for c in range(2)
        ],
    )
    near_peer = fetch(near_own, "core", 1)
    back, _ = lax.optimization_barrier((back, (weight, border)))
    back = lax.all_to_all(back, "z", 0, 0, tiled=True)
    keep, give, weight = call(
        attention_kernel,
        [((4, 128, 128), BF16), ((4, 128, 128), BF16), ((1024, 128), BF16)],
        [SMEM] + [VMEM] * 8,
        "attention",
        scratch=[
            pltpu.VMEM((1024, 128), BF16),
            pltpu.VMEM((1024 + 2 * WIN, 256), BF16),
            pltpu.VMEM((2, 4, 128, 128), BF16),
        ],
    )(at, own, peer, weight, near_own, near_peer, qk_gain, first, count)

    right, left = fetch(back, "x", 1), fetch(back, "x", 3)
    up_far = fetch(right[:, :, :512], "x", 1)
    down_far = fetch(left[:, :, 512:], "x", 3)

    out_peer = fetch(weight, "core", 1)
    got = fetch(give, "core", 1)
    mine_attended, away = call(
        project_kernel,
        [((128, 1024), F32), ((3, 128, 1024), BF16)],
        [SMEM] + [VMEM] * 4,
        "project",
    )(at, keep, got, weight, out_peer)
    parts = [fetch(away[k - 1], "y", 4 - k) for k in (2, 1, 3)]
    middle, normed_two = call(
        middle_kernel,
        [((128, 1024), BF16)] * 2,
        [VMEM] * 6,
        "middle",
    )(tokens, mine_attended, *parts, norm2_gain.reshape(1, 1024))

    far = {k: fetch(normed_two, "y", k) for k in (2, 1, 3)}
    laid, far = lax.optimization_barrier(((back, right, up_far, down_far, left), far))
    (mlp_own,) = call(lay_kernel, [((1024, 1024), BF16)], [SMEM] + [VMEM] * 5, "mlp_lay")(
        at, *laid
    )
    mlp_peer = fetch(mlp_own, "core", 1)
    (part,) = call(mlp_first_kernel, [((512, 1024), F32)], [VMEM] * 5, "mlp_first", mib=16)(
        normed_two, far[1], far[2], far[3], mlp_own
    )
    parts = [fetch(mlp_second(far[k], mlp_peer, part, k), "y", 4 - k) for k in (2, 1, 3)]
    mine = mlp_second(normed_two, mlp_peer, part, 0)
    (out,) = call(end_kernel, [((128, 1024), BF16)], [VMEM] * 5, "end")(middle, mine, *parts)
    return out


def solution(mesh):
    fine = Mesh(mesh.devices.reshape(8, 4, 4, 2), ("z", "x", "y", "core"))
    seq, head = ("z", "x"), ("y", "core")
    return jax.shard_map(
        local,
        mesh=fine,
        in_specs=(
            P(seq + head, None),
            P(seq),
            P(seq),
            P(),
            P(seq, None, head),
            P(None, head, None),
            P(head, seq),
            P(),
            P(seq, head),
            P(head, seq),
        ),
        out_specs=P(seq + head, None),
        check_vma=False,
    )
```

```python
import functools

import jax
import jax.numpy as jnp
from jax import lax
from jax.experimental import pallas as pl
from jax.experimental.pallas import tpu as pltpu
from jax.sharding import Mesh, PartitionSpec as P

WIN = 64
F32, BF16 = jnp.float32, jnp.bfloat16
NT = (((1,), (1,)), ((), ()))
VMEM = pl.BlockSpec(memory_space=pltpu.VMEM)
HBM = pl.BlockSpec(memory_space=pltpu.HBM)
SMEM = pl.BlockSpec(memory_space=pltpu.SMEM)


def params(mib):
    return pltpu.CompilerParams(vmem_limit_bytes=mib * 2**20)


def layer_norm(values, gain):
    center = values - jnp.mean(values, axis=-1, keepdims=True)
    spread = jnp.mean(center * center, axis=-1, keepdims=True)
    return (center * lax.rsqrt(spread + 1e-06) * gain).astype(BF16)


def head_norm(values, gain, half):
    square = values * values
    low = jnp.sum(jnp.where(half, square, 0.0), axis=-1, keepdims=True)
    high = jnp.sum(jnp.where(half, 0.0, square), axis=-1, keepdims=True)
    scale = lax.rsqrt(jnp.where(half, low, high) * (1.0 / 64) + 1e-06)
    return (values * scale * gain).astype(BF16)


def first_half(rows):
    return lax.broadcasted_iota(jnp.int32, (rows, 128), 1) < 64


def start_kernel(*refs):
    held, (normed, front, back), here, sems = refs[:6], refs[6:9], refs[9:15], refs[15]
    copies = [
        pltpu.make_async_copy(a, b, sems.at[i]) for i, (a, b) in enumerate(zip(held, here))
    ]
    for copy in copies:
        copy.start()
    qkv, out_t, tok, gain, up, down_t = here
    copies[0].wait()
    copies[1].wait()
    pack = jnp.concatenate([qkv[0], qkv[1], qkv[2], out_t[...]], axis=1)
    for i in range(8):
        front[i] = pack
    copies[2].wait()
    copies[3].wait()
    normed[...] = layer_norm(tok[...].astype(F32), gain[...])
    copies[4].wait()
    copies[5].wait()
    pack = jnp.concatenate([up[...], down_t[...]], axis=1)
    for i in range(8):
        back[i] = pack


def collect_kernel(at, *refs):
    blocks, own, border = refs[:4], refs[4:6], refs[6]
    y, core = at[0], at[1]
    for k in range(4):
        t = lax.rem(y + k, 4)
        for low in range(2):

            @pl.when(t // 2 == low)
            def _():
                own[low][lax.rem(t, 2)] = blocks[k][...]

        @pl.when((core == 0) & (t == 0))
        def _():
            border[...] = blocks[k][:WIN]

        @pl.when((core == 1) & (t == 3))
        def _():
            border[...] = blocks[k][128 - WIN :]


def lay(x, here, right, far_low, far_high, left, out):
    half = out.shape[1] // 2
    for k, block in enumerate((here, right, None, left)):
        base = lax.rem(x + k, 4) * 32
        for z in range(8):
            rows = pl.ds(pl.multiple_of(z * 128 + base, 32), 32)
            if block is None:
                out[rows, :half] = far_low[z]
                out[rows, half:] = far_high[z]
            else:
                out[rows] = block[z]


def lay_kernel(at, *refs):
    lay(at[2], *refs)


def attend(query, kv, first, count, key_start):
    lower = jnp.broadcast_to(first, (128, 128)).T
    upper = lower + jnp.broadcast_to(count, (128, 128)).T
    index = key_start + lax.broadcasted_iota(jnp.int32, (128, 256), 1)
    lower = jnp.concatenate([lower, lower], axis=1)
    upper = jnp.concatenate([upper, upper], axis=1)
    allowed = (index >= lower) & (index < upper)
    outs = []
    for h in range(2):
        lanes = slice(h * 64, h * 64 + 64)
        score = lax.dot_general(query[:, lanes], kv[:, lanes], NT, preferred_element_type=F32)
        weight = jnp.where(allowed, jnp.exp(score * 0.125), 0.0)
        total = jnp.sum(weight, axis=-1, keepdims=True)
        prob = (weight / total).astype(BF16)
        value = kv[:, 128 + h * 64 : 192 + h * 64]
        outs.append(jnp.dot(prob, value, preferred_element_type=F32))
    return jnp.concatenate(outs, axis=1).astype(BF16)


def attention_kernel(
    at, own_low, own_high, peer_low, peer_high, here, right, far_low, far_high, left,
    near_own, near_peer, gains, first, count, keep, give, out_w, weight, q_s, kv_s, att,
):
    lay(at[2], here, right, far_low, far_high, left, weight)
    core, anchor = at[1], at[3]
    gain = gains[...]
    gain = jnp.concatenate([gain[:, 0], gain[:, 1]], axis=1)
    out_w[...] = weight[:, 384:]

    rows = jnp.concatenate([near_own[...], near_peer[...]], axis=0)
    part = jnp.dot(rows, weight[:, 128:384], preferred_element_type=F32)
    key = head_norm(part[:, :128], gain[1:2], first_half(2 * WIN))
    kv = jnp.concatenate([key, part[:, 128:].astype(BF16)], axis=1)
    end = WIN + 1024
    kv_s[pl.ds(pl.multiple_of((1 - core) * end, WIN), WIN)] = kv[:WIN]
    kv_s[pl.ds(pl.multiple_of(core * end, WIN), WIN)] = kv[WIN:]

    half = first_half(256)
    for t in range(4):
        other = peer_low[t] if t < 2 else peer_high[t - 2]
        rows = jnp.concatenate([own_low[t] if t < 2 else own_high[t - 2], other], axis=0)
        qkv = jnp.dot(rows, weight[:, :384], preferred_element_type=F32)
        query = head_norm(qkv[:, :128], gain[0:1], half)
        key = head_norm(qkv[:, 128:256], gain[1:2], half)
        kv = jnp.concatenate([key, qkv[:, 256:].astype(BF16)], axis=1)
        mine = pl.multiple_of(t * 256 + core * 128, 128)
        theirs = pl.multiple_of(t * 256 + (1 - core) * 128, 128)
        q_s[pl.ds(mine, 128)] = query[:128]
        q_s[pl.ds(theirs, 128)] = query[128:]
        kv_s[pl.ds(pl.multiple_of(mine + WIN, WIN), 128)] = kv[:128]
        kv_s[pl.ds(pl.multiple_of(theirs + WIN, WIN), 128)] = kv[128:]
    for b in range(8):
        att[lax.rem(core + b, 2), b // 2] = attend(
            q_s[b * 128 : b * 128 + 128],
            kv_s[b * 128 : b * 128 + 256],
            first[b : b + 1],
            count[b : b + 1],
            anchor + (b * 128 - WIN),
        )
    keep[...] = att[0]
    give[...] = att[1]


def project_kernel(at, keep, got, weight, other, mine, away):
    y = at[0]
    rows = jnp.concatenate(
        [keep[...].reshape(512, 128), got[...].reshape(512, 128)], axis=1
    )
    both = jnp.concatenate([weight[...], other[...]], axis=1)
    part = lax.dot_general(rows, both, NT, preferred_element_type=F32)
    for t in range(4):
        block = part[t * 128 : t * 128 + 128]

        @pl.when(y == t)
        def _():
            mine[...] = block

        @pl.when(y != t)
        def _():
            away[lax.rem(t + 3 - y, 4)] = block.astype(BF16)


def middle_kernel(tok, mine, a, b, c, gain, middle, normed):
    total = mine[...] + a[...].astype(F32) + b[...].astype(F32) + c[...].astype(F32)
    mid = (tok[...].astype(F32) + total).astype(BF16)
    middle[...] = mid
    normed[...] = layer_norm(mid.astype(F32), gain[...])


def hidden_share(rows, weight):
    hidden = jax.nn.gelu(
        jnp.dot(rows, weight[:, :512], preferred_element_type=F32), approximate=True
    ).astype(BF16)
    return lax.dot_general(hidden, weight[:, 512:], NT, preferred_element_type=F32)


def mlp_first_kernel(a, b, c, d, weight, out):
    rows = jnp.concatenate([a[...], b[...], c[...], d[...]], axis=0)
    out[...] = hidden_share(rows, weight)


def mlp_second_kernel(rows, weight, part, out, *, at):
    total = part[at * 128 : at * 128 + 128] + hidden_share(rows[...], weight)
    out[...] = total.astype(out.dtype)


def mlp_second(rows, weight, part, at):
    return call(
        functools.partial(mlp_second_kernel, at=at),
        [((128, 1024), F32 if at == 0 else BF16)],
        [VMEM] * 3,
        "mlp_second",
    )(rows, weight, part)[0]


def end_kernel(middle, mine, a, b, c, out):
    total = middle[...].astype(F32) + mine[...]
    total += a[...].astype(F32) + b[...].astype(F32) + c[...].astype(F32)
    out[...] = total.astype(BF16)


def call(kernel, outs, specs, name, mib=8, scratch=(), flops=2**20, **more):
    return pl.pallas_call(
        kernel,
        out_shape=[jax.ShapeDtypeStruct(s, d) for s, d in outs],
        in_specs=specs,
        out_specs=[VMEM] * len(outs),
        scratch_shapes=list(scratch),
        compiler_params=params(mib),
        cost_estimate=pl.CostEstimate(flops=flops, bytes_accessed=2**21, transcendentals=0),
        name=name,
        **more,
    )


def fetch(value, axis, step):
    n = lax.axis_size(axis)
    return lax.ppermute(value, axis, [((i + step) % n, i) for i in range(n)])


def relay(block):
    half = block.shape[2] // 2
    right, left = fetch(block, "x", 1), fetch(block, "x", 3)
    far_low, far_high = fetch(right[:, :, :half], "x", 1), fetch(left[:, :, half:], "x", 3)
    return block, right, far_low, far_high, left


def local(
    tokens,
    win_first,
    win_count,
    norm1_gain,
    qkv_weight,
    qk_gain,
    out_weight,
    norm2_gain,
    up_weight,
    down_weight,
):
    y, core = lax.axis_index("y"), lax.axis_index("core")
    seq = lax.axis_index("z") * lax.axis_size("x") + lax.axis_index("x")
    at = jnp.stack([y, core, lax.axis_index("x"), seq * 1024]).astype(jnp.int32)
    first, count = win_first.reshape(8, 128), win_count.reshape(8, 128)

    given = [
        jnp.transpose(qkv_weight, (1, 0, 2)),
        out_weight.T,
        tokens,
        norm1_gain.reshape(1, 1024),
        up_weight,
        down_weight.T,
    ]
    normed, front, back = call(
        start_kernel,
        [((128, 1024), BF16), ((8, 32, 512), BF16), ((8, 32, 1024), BF16)],
        [HBM] * 6,
        "start",
        scratch=[pltpu.VMEM(v.shape, v.dtype) for v in given]
        + [pltpu.SemaphoreType.DMA((6,))],
    )(*[pltpu.with_memory_space_constraint(v, pltpu.HBM) for v in given])
    front = lax.all_to_all(front, "z", 0, 0, tiled=True)
    far = {k: fetch(normed, "y", k) for k in (2, 1, 3)}
    weights = relay(front)
    back, _ = lax.optimization_barrier((back, front))
    back = lax.all_to_all(back, "z", 0, 0, tiled=True)
    far, _ = lax.optimization_barrier((far, (weights[1], weights[4])))
    own_low, own_high, border = call(
        collect_kernel,
        [((2, 128, 1024), BF16), ((2, 128, 1024), BF16), ((WIN, 1024), BF16)],
        [SMEM] + [VMEM] * 4,
        "collect",
    )(at, normed, far[1], far[2], far[3])
    peer_low, peer_high = fetch(own_low, "core", 1), fetch(own_high, "core", 1)
    spot = lambda z, x, y, core: ((z * 4 + x) * 4 + y) * 2 + core
    shift = lambda s, by: divmod((s + by) % 32, 4)
    near_own = lax.ppermute(
        border,
        ("z", "x", "y", "core"),
        [
            (spot(*divmod(s, 4), j, c), spot(*shift(s, 2 * c - 1), j, c))
            for s in range(32)
            for j in range(4)
            for c in range(2)
        ],
    )
    near_peer = fetch(near_own, "core", 1)
    keep, give, weight = call(
        attention_kernel,
        [((4, 128, 128), BF16), ((4, 128, 128), BF16), ((1024, 128), BF16)],
        [SMEM] + [VMEM] * 14,
        "attention",
        scratch=[
            pltpu.VMEM((1024, 512), BF16),
            pltpu.VMEM((1024, 128), BF16),
            pltpu.VMEM((1024 + 2 * WIN, 256), BF16),
            pltpu.VMEM((2, 4, 128, 128), BF16),
        ],
    )(at, own_low, own_high, peer_low, peer_high, *weights, near_own, near_peer, qk_gain, first, count)

    mlp_weights = relay(back)
    out_peer = fetch(weight, "core", 1)
    got = fetch(give, "core", 1)
    mine_attended, away = call(
        project_kernel,
        [((128, 1024), F32), ((3, 128, 1024), BF16)],
        [SMEM] + [VMEM] * 4,
        "project",
    )(at, keep, got, weight, out_peer)
    parts = [fetch(away[k - 1], "y", 4 - k) for k in (2, 1, 3)]
    middle, normed_two = call(
        middle_kernel,
        [((128, 1024), BF16)] * 2,
        [VMEM] * 6,
        "middle",
    )(tokens, mine_attended, *parts, norm2_gain.reshape(1, 1024))

    far = {k: fetch(normed_two, "y", k) for k in (2, 1, 3)}
    laid, far = lax.optimization_barrier((mlp_weights, far))
    (mlp_own,) = call(lay_kernel, [((1024, 1024), BF16)], [SMEM] + [VMEM] * 5, "mlp_lay")(
        at, *laid
    )
    mlp_peer = fetch(mlp_own, "core", 1)
    (part,) = call(mlp_first_kernel, [((512, 1024), F32)], [VMEM] * 5, "mlp_first", mib=16)(
        normed_two, far[1], far[2], far[3], mlp_own
    )
    parts = [fetch(mlp_second(far[k], mlp_peer, part, k), "y", 4 - k) for k in (2, 1, 3)]
    mine = mlp_second(normed_two, mlp_peer, part, 0)
    (out,) = call(end_kernel, [((128, 1024), BF16)], [VMEM] * 5, "end")(middle, mine, *parts)
    return out


def solution(mesh):
    fine = Mesh(mesh.devices.reshape(8, 4, 4, 2), ("z", "x", "y", "core"))
    seq, head = ("z", "x"), ("y", "core")
    return jax.shard_map(
        local,
        mesh=fine,
        in_specs=(
            P(seq + head, None),
            P(seq),
            P(seq),
            P(),
            P(seq, None, head),
            P(None, head, None),
            P(head, seq),
            P(),
            P(seq, head),
            P(head, seq),
        ),
        out_specs=P(seq + head, None),
        check_vma=False,
    )
```

```python
import functools

import jax
import jax.numpy as jnp
from jax import lax
from jax.experimental import pallas as pl
from jax.experimental.pallas import tpu as pltpu
from jax.sharding import Mesh, PartitionSpec as P

WIN = 64
F32, BF16 = jnp.float32, jnp.bfloat16
NT = (((1,), (1,)), ((), ()))
VMEM = pl.BlockSpec(memory_space=pltpu.VMEM)
HBM = pl.BlockSpec(memory_space=pltpu.HBM)
SMEM = pl.BlockSpec(memory_space=pltpu.SMEM)


def params(mib):
    return pltpu.CompilerParams(vmem_limit_bytes=mib * 2**20)


def layer_norm(values, gain):
    center = values - jnp.mean(values, axis=-1, keepdims=True)
    spread = jnp.mean(center * center, axis=-1, keepdims=True)
    return (center * lax.rsqrt(spread + 1e-06) * gain).astype(BF16)


def head_norm(values, gain, half):
    square = values * values
    low = jnp.sum(jnp.where(half, square, 0.0), axis=-1, keepdims=True)
    high = jnp.sum(jnp.where(half, 0.0, square), axis=-1, keepdims=True)
    scale = lax.rsqrt(jnp.where(half, low, high) * (1.0 / 64) + 1e-06)
    return (values * scale * gain).astype(BF16)


def first_half(rows):
    return lax.broadcasted_iota(jnp.int32, (rows, 128), 1) < 64


def bring(held, here, sems):
    copies = [
        pltpu.make_async_copy(a, b, sems.at[i]) for i, (a, b) in enumerate(zip(held, here))
    ]
    for copy in copies:
        copy.start()
    return copies


def pack_kernel(*refs):
    held, front, here, sems = refs[:2], refs[2], refs[3:5], refs[5]
    for copy in bring(held, here, sems):
        copy.wait()
    qkv, out_t = here
    pack = jnp.concatenate([qkv[0], qkv[1], qkv[2], out_t[...]], axis=1)
    for i in range(8):
        front[i] = pack


def start_kernel(*refs):
    held, (normed, back), here, sems = refs[:4], refs[4:6], refs[6:10], refs[10]
    copies = bring(held, here, sems)
    tok, gain, up, down_t = here
    copies[0].wait()
    copies[1].wait()
    normed[...] = layer_norm(tok[...].astype(F32), gain[...])
    copies[2].wait()
    copies[3].wait()
    pack = jnp.concatenate([up[...], down_t[...]], axis=1)
    for i in range(8):
        back[i] = pack


def from_hbm(kernel, outs, given, name):
    return call(
        kernel,
        outs,
        [HBM] * len(given),
        name,
        scratch=[pltpu.VMEM(v.shape, v.dtype) for v in given]
        + [pltpu.SemaphoreType.DMA((len(given),))],
    )(*[pltpu.with_memory_space_constraint(v, pltpu.HBM) for v in given])


def collect_kernel(at, *refs):
    blocks, own, border = refs[:4], refs[4:6], refs[6]
    y, core = at[0], at[1]
    for k in range(4):
        t = lax.rem(y + k, 4)
        for low in range(2):

            @pl.when(t // 2 == low)
            def _():
                own[low][lax.rem(t, 2)] = blocks[k][...]

        @pl.when((core == 0) & (t == 0))
        def _():
            border[...] = blocks[k][:WIN]

        @pl.when((core == 1) & (t == 3))
        def _():
            border[...] = blocks[k][128 - WIN :]


def lay(x, here, right, far_low, far_high, left, out):
    half = out.shape[1] // 2
    for k, block in enumerate((here, right, None, left)):
        base = lax.rem(x + k, 4) * 32
        for z in range(8):
            rows = pl.ds(pl.multiple_of(z * 128 + base, 32), 32)
            if block is None:
                out[rows, :half] = far_low[z]
                out[rows, half:] = far_high[z]
            else:
                out[rows] = block[z]


def lay_kernel(at, *refs):
    lay(at[2], *refs)


def attend(query, kv, first, count, key_start):
    lower = jnp.broadcast_to(first, (128, 128)).T
    upper = lower + jnp.broadcast_to(count, (128, 128)).T
    index = key_start + lax.broadcasted_iota(jnp.int32, (128, 256), 1)
    lower = jnp.concatenate([lower, lower], axis=1)
    upper = jnp.concatenate([upper, upper], axis=1)
    allowed = (index >= lower) & (index < upper)
    outs = []
    for h in range(2):
        lanes = slice(h * 64, h * 64 + 64)
        score = lax.dot_general(query[:, lanes], kv[:, lanes], NT, preferred_element_type=F32)
        weight = jnp.where(allowed, jnp.exp(score * 0.125), 0.0)
        total = jnp.sum(weight, axis=-1, keepdims=True)
        prob = (weight * (1.0 / total)).astype(BF16)
        value = kv[:, 128 + h * 64 : 192 + h * 64]
        outs.append(jnp.dot(prob, value, preferred_element_type=F32))
    return jnp.concatenate(outs, axis=1).astype(BF16)


def attention_kernel(
    at, own_low, own_high, peer_low, peer_high, here, right, far_low, far_high, left,
    near_own, near_peer, gains, first, count, keep, give, out_w, weight, q_s, kv_s, att,
):
    lay(at[2], here, right, far_low, far_high, left, weight)
    core, anchor = at[1], at[3]
    gain = gains[...]
    gain = jnp.concatenate([gain[:, 0], gain[:, 1]], axis=1)
    out_w[...] = weight[:, 384:]

    rows = jnp.concatenate([near_own[...], near_peer[...]], axis=0)
    part = jnp.dot(rows, weight[:, 128:384], preferred_element_type=F32)
    key = head_norm(part[:, :128], gain[1:2], first_half(2 * WIN))
    kv = jnp.concatenate([key, part[:, 128:].astype(BF16)], axis=1)
    end = WIN + 1024
    kv_s[pl.ds(pl.multiple_of((1 - core) * end, WIN), WIN)] = kv[:WIN]
    kv_s[pl.ds(pl.multiple_of(core * end, WIN), WIN)] = kv[WIN:]

    half = first_half(512)
    for low, (own, peer) in enumerate(((own_low, peer_low), (own_high, peer_high))):
        rows = jnp.concatenate([own[0], own[1], peer[0], peer[1]], axis=0)
        qkv = jnp.dot(rows, weight[:, :384], preferred_element_type=F32)
        query = head_norm(qkv[:, :128], gain[0:1], half)
        key = head_norm(qkv[:, 128:256], gain[1:2], half)
        kv = jnp.concatenate([key, qkv[:, 256:].astype(BF16)], axis=1)
        for i in range(4):
            place = core if i < 2 else 1 - core
            row = pl.multiple_of(low * 512 + i % 2 * 256 + place * 128, 128)
            q_s[pl.ds(row, 128)] = query[i * 128 : i * 128 + 128]
            kv_s[pl.ds(pl.multiple_of(row + WIN, WIN), 128)] = kv[i * 128 : i * 128 + 128]
    for b in range(8):
        att[lax.rem(core + b, 2), b // 2] = attend(
            q_s[b * 128 : b * 128 + 128],
            kv_s[b * 128 : b * 128 + 256],
            first[b : b + 1],
            count[b : b + 1],
            anchor + (b * 128 - WIN),
        )
    keep[...] = att[0]
    give[...] = att[1]


def project_kernel(at, keep, got, weight, other, mine, away):
    y = at[0]
    rows = jnp.concatenate(
        [keep[...].reshape(512, 128), got[...].reshape(512, 128)], axis=1
    )
    both = jnp.concatenate([weight[...], other[...]], axis=1)
    part = lax.dot_general(rows, both, NT, preferred_element_type=F32)
    for t in range(4):
        block = part[t * 128 : t * 128 + 128]

        @pl.when(y == t)
        def _():
            mine[...] = block

        @pl.when(y != t)
        def _():
            away[lax.rem(t + 3 - y, 4)] = block.astype(BF16)


def middle_kernel(tok, mine, a, b, c, gain, middle, normed):
    total = mine[...] + a[...].astype(F32) + b[...].astype(F32) + c[...].astype(F32)
    mid = (tok[...].astype(F32) + total).astype(BF16)
    middle[...] = mid
    normed[...] = layer_norm(mid.astype(F32), gain[...])


def hidden_share(rows, weight):
    hidden = jax.nn.gelu(
        jnp.dot(rows, weight[:, :512], preferred_element_type=F32), approximate=True
    ).astype(BF16)
    return lax.dot_general(hidden, weight[:, 512:], NT, preferred_element_type=F32)


def mlp_first_kernel(a, b, c, d, weight, out):
    rows = jnp.concatenate([a[...], b[...], c[...], d[...]], axis=0)
    out[...] = hidden_share(rows, weight)


def mlp_second_kernel(rows, weight, part, out, *, at):
    total = part[at * 128 : at * 128 + 128] + hidden_share(rows[...], weight)
    out[...] = total.astype(out.dtype)


def mlp_second(rows, weight, part, at):
    return call(
        functools.partial(mlp_second_kernel, at=at),
        [((128, 1024), F32 if at == 0 else BF16)],
        [VMEM] * 3,
        "mlp_second",
    )(rows, weight, part)[0]


def end_kernel(middle, mine, a, b, c, out):
    total = middle[...].astype(F32) + mine[...]
    total += a[...].astype(F32) + b[...].astype(F32) + c[...].astype(F32)
    out[...] = total.astype(BF16)


def call(kernel, outs, specs, name, mib=8, scratch=(), flops=2**20, **more):
    return pl.pallas_call(
        kernel,
        out_shape=[jax.ShapeDtypeStruct(s, d) for s, d in outs],
        in_specs=specs,
        out_specs=[VMEM] * len(outs),
        scratch_shapes=list(scratch),
        compiler_params=params(mib),
        cost_estimate=pl.CostEstimate(flops=flops, bytes_accessed=2**21, transcendentals=0),
        name=name,
        **more,
    )


def fetch(value, axis, step):
    n = lax.axis_size(axis)
    return lax.ppermute(value, axis, [((i + step) % n, i) for i in range(n)])


def relay(block):
    half = block.shape[2] // 2
    right, left = fetch(block, "x", 1), fetch(block, "x", 3)
    far_low, far_high = fetch(right[:, :, :half], "x", 1), fetch(left[:, :, half:], "x", 3)
    return block, right, far_low, far_high, left


def local(
    tokens,
    win_first,
    win_count,
    norm1_gain,
    qkv_weight,
    qk_gain,
    out_weight,
    norm2_gain,
    up_weight,
    down_weight,
):
    y, core = lax.axis_index("y"), lax.axis_index("core")
    seq = lax.axis_index("z") * lax.axis_size("x") + lax.axis_index("x")
    at = jnp.stack([y, core, lax.axis_index("x"), seq * 1024]).astype(jnp.int32)
    first, count = win_first.reshape(8, 128), win_count.reshape(8, 128)

    (front,) = from_hbm(
        pack_kernel,
        [((8, 32, 512), BF16)],
        [jnp.transpose(qkv_weight, (1, 0, 2)), out_weight.T],
        "pack",
    )
    normed, back = from_hbm(
        start_kernel,
        [((128, 1024), BF16), ((8, 32, 1024), BF16)],
        [tokens, norm1_gain.reshape(1, 1024), up_weight, down_weight.T],
        "start",
    )
    front = lax.all_to_all(front, "z", 0, 0, tiled=True)
    far = {k: fetch(normed, "y", k) for k in (1, 3, 2)}
    weights = relay(front)
    back, _ = lax.optimization_barrier((back, front))
    back = lax.all_to_all(back, "z", 0, 0, tiled=True)
    far, _ = lax.optimization_barrier((far, (weights[1], weights[4])))
    own_low, own_high, border = call(
        collect_kernel,
        [((2, 128, 1024), BF16), ((2, 128, 1024), BF16), ((WIN, 1024), BF16)],
        [SMEM] + [VMEM] * 4,
        "collect",
    )(at, normed, far[1], far[2], far[3])
    peer_low, peer_high = fetch(own_low, "core", 1), fetch(own_high, "core", 1)
    spot = lambda z, x, y, core: ((z * 4 + x) * 4 + y) * 2 + core
    shift = lambda s, by: divmod((s + by) % 32, 4)
    near_own = lax.ppermute(
        border,
        ("z", "x", "y", "core"),
        [
            (spot(*divmod(s, 4), j, c), spot(*shift(s, 2 * c - 1), j, c))
            for s in range(32)
            for j in range(4)
            for c in range(2)
        ],
    )
    near_peer = fetch(near_own, "core", 1)
    keep, give, weight = call(
        attention_kernel,
        [((4, 128, 128), BF16), ((4, 128, 128), BF16), ((1024, 128), BF16)],
        [SMEM] + [VMEM] * 14,
        "attention",
        scratch=[
            pltpu.VMEM((1024, 512), BF16),
            pltpu.VMEM((1024, 128), BF16),
            pltpu.VMEM((1024 + 2 * WIN, 256), BF16),
            pltpu.VMEM((2, 4, 128, 128), BF16),
        ],
    )(at, own_low, own_high, peer_low, peer_high, *weights, near_own, near_peer, qk_gain, first, count)

    mlp_weights = relay(back)
    out_peer = fetch(weight, "core", 1)
    got = fetch(give, "core", 1)
    mine_attended, away = call(
        project_kernel,
        [((128, 1024), F32), ((3, 128, 1024), BF16)],
        [SMEM] + [VMEM] * 4,
        "project",
    )(at, keep, got, weight, out_peer)
    parts = [fetch(away[k - 1], "y", 4 - k) for k in (1, 3, 2)]
    middle, normed_two = call(
        middle_kernel,
        [((128, 1024), BF16)] * 2,
        [VMEM] * 6,
        "middle",
    )(tokens, mine_attended, *parts, norm2_gain.reshape(1, 1024))

    far = {k: fetch(normed_two, "y", k) for k in (1, 3, 2)}
    laid, far = lax.optimization_barrier((mlp_weights, far))
    (mlp_own,) = call(lay_kernel, [((1024, 1024), BF16)], [SMEM] + [VMEM] * 5, "mlp_lay")(
        at, *laid
    )
    mlp_peer = fetch(mlp_own, "core", 1)
    (part,) = call(mlp_first_kernel, [((512, 1024), F32)], [VMEM] * 5, "mlp_first", mib=16)(
        normed_two, far[1], far[2], far[3], mlp_own
    )
    parts = [fetch(mlp_second(far[k], mlp_peer, part, k), "y", 4 - k) for k in (1, 3, 2)]
    mine = mlp_second(normed_two, mlp_peer, part, 0)
    (out,) = call(end_kernel, [((128, 1024), BF16)], [VMEM] * 5, "end")(middle, mine, *parts)
    return out


def solution(mesh):
    fine = Mesh(mesh.devices.reshape(8, 4, 4, 2), ("z", "x", "y", "core"))
    seq, head = ("z", "x"), ("y", "core")
    return jax.shard_map(
        local,
        mesh=fine,
        in_specs=(
            P(seq + head, None),
            P(seq),
            P(seq),
            P(),
            P(seq, None, head),
            P(None, head, None),
            P(head, seq),
            P(),
            P(seq, head),
            P(head, seq),
        ),
        out_specs=P(seq + head, None),
        check_vma=False,
    )
```

```python
import functools

import jax
import jax.numpy as jnp
from jax import lax
from jax.experimental import pallas as pl
from jax.experimental.pallas import tpu as pltpu
from jax.sharding import Mesh, PartitionSpec as P

WIN = 64
F32, BF16 = jnp.float32, jnp.bfloat16
NT = (((1,), (1,)), ((), ()))
VMEM = pl.BlockSpec(memory_space=pltpu.VMEM)
HBM = pl.BlockSpec(memory_space=pltpu.HBM)
SMEM = pl.BlockSpec(memory_space=pltpu.SMEM)


def params(mib):
    return pltpu.CompilerParams(vmem_limit_bytes=mib * 2**20)


def layer_norm(values, gain):
    center = values - jnp.mean(values, axis=-1, keepdims=True)
    spread = jnp.mean(center * center, axis=-1, keepdims=True)
    return (center * lax.rsqrt(spread + 1e-06) * gain).astype(BF16)


def head_norm(values, gain, half):
    square = values * values
    low = jnp.sum(jnp.where(half, square, 0.0), axis=-1, keepdims=True)
    high = jnp.sum(jnp.where(half, 0.0, square), axis=-1, keepdims=True)
    scale = lax.rsqrt(jnp.where(half, low, high) * (1.0 / 64) + 1e-06)
    return (values * scale * gain).astype(BF16)


def first_half(rows):
    return lax.broadcasted_iota(jnp.int32, (rows, 128), 1) < 64


def bring(held, here, sems):
    copies = [
        pltpu.make_async_copy(a, b, sems.at[i]) for i, (a, b) in enumerate(zip(held, here))
    ]
    for copy in copies:
        copy.start()
    return copies


def pack_kernel(*refs):
    held, front, here, sems = refs[:2], refs[2], refs[3:5], refs[5]
    for copy in bring(held, here, sems):
        copy.wait()
    qkv, out_t = here
    pack = jnp.concatenate([qkv[0], qkv[1], qkv[2], out_t[...]], axis=1)
    for i in range(8):
        front[i] = pack


def norm_kernel(*refs):
    held, normed, here, sems = refs[:2], refs[2], refs[3:5], refs[5]
    for copy in bring(held, here, sems):
        copy.wait()
    tok, gain = here
    normed[...] = layer_norm(tok[...].astype(F32), gain[...])


def mlp_pack_kernel(*refs):
    held, back, here, sems = refs[:2], refs[2], refs[3:5], refs[5]
    for copy in bring(held, here, sems):
        copy.wait()
    up, down_t = here
    pack = jnp.concatenate([up[...], down_t[...]], axis=1)
    for i in range(8):
        back[i] = pack


def from_hbm(kernel, outs, given, name):
    return call(
        kernel,
        outs,
        [HBM] * len(given),
        name,
        scratch=[pltpu.VMEM(v.shape, v.dtype) for v in given]
        + [pltpu.SemaphoreType.DMA((len(given),))],
    )(*[pltpu.with_memory_space_constraint(v, pltpu.HBM) for v in given])


def collect_kernel(at, *refs):
    blocks, own, border = refs[:4], refs[4:6], refs[6]
    y, core = at[0], at[1]
    for k in range(4):
        t = lax.rem(y + k, 4)
        for low in range(2):

            @pl.when(t // 2 == low)
            def _():
                own[low][lax.rem(t, 2)] = blocks[k][...]

        @pl.when((core == 0) & (t == 0))
        def _():
            border[...] = blocks[k][:WIN]

        @pl.when((core == 1) & (t == 3))
        def _():
            border[...] = blocks[k][128 - WIN :]


def lay(x, here, right, far_low, far_high, left, out):
    half = out.shape[1] // 2
    for k, block in enumerate((here, right, None, left)):
        base = lax.rem(x + k, 4) * 32
        for z in range(8):
            rows = pl.ds(pl.multiple_of(z * 128 + base, 32), 32)
            if block is None:
                out[rows, :half] = far_low[z]
                out[rows, half:] = far_high[z]
            else:
                out[rows] = block[z]


def lay_kernel(at, *refs):
    lay(at[2], *refs)


def attend(query, kv, first, count, key_start):
    lower = jnp.broadcast_to(first, (128, 128)).T
    upper = lower + jnp.broadcast_to(count, (128, 128)).T
    index = key_start + lax.broadcasted_iota(jnp.int32, (128, 256), 1)
    lower = jnp.concatenate([lower, lower], axis=1)
    upper = jnp.concatenate([upper, upper], axis=1)
    allowed = (index >= lower) & (index < upper)
    low = first_half(128)
    values = kv[:, 128:]
    one, none = jnp.ones_like(values), jnp.zeros_like(query)
    pick = first_half(256)
    sums = []
    for h in range(2):
        own = low if h == 0 else ~low
        score = lax.dot_general(
            jnp.where(own, query, none), kv[:, :128], NT, preferred_element_type=F32
        )
        weight = jnp.where(allowed, jnp.exp(score * 0.125), 0.0).astype(BF16)
        held = jnp.where(pick if h == 0 else ~pick, values, one)
        sums.append(jnp.dot(weight, held, preferred_element_type=F32))
    mixed = jnp.where(low, sums[0], sums[1])
    total = pltpu.roll(jnp.where(low, sums[1], sums[0]), 64, 1)
    return (mixed / total).astype(BF16)


def attention_kernel(
    at, own_low, own_high, peer_low, peer_high, here, right, far_low, far_high, left,
    near_own, near_peer, gains, first, count, keep, give, out_w, weight, q_s, kv_s, att,
):
    lay(at[2], here, right, far_low, far_high, left, weight)
    core, anchor = at[1], at[3]
    gain = gains[...]
    gain = jnp.concatenate([gain[:, 0], gain[:, 1]], axis=1)
    out_w[...] = weight[:, 384:]

    rows = jnp.concatenate([near_own[...], near_peer[...]], axis=0)
    part = jnp.dot(rows, weight[:, 128:384], preferred_element_type=F32)
    key = head_norm(part[:, :128], gain[1:2], first_half(2 * WIN))
    kv = jnp.concatenate([key, part[:, 128:].astype(BF16)], axis=1)
    end = WIN + 1024
    kv_s[pl.ds(pl.multiple_of((1 - core) * end, WIN), WIN)] = kv[:WIN]
    kv_s[pl.ds(pl.multiple_of(core * end, WIN), WIN)] = kv[WIN:]

    half = first_half(512)
    for low, (own, peer) in enumerate(((own_low, peer_low), (own_high, peer_high))):
        rows = jnp.concatenate([own[0], own[1], peer[0], peer[1]], axis=0)
        qkv = jnp.dot(rows, weight[:, :384], preferred_element_type=F32)
        query = head_norm(qkv[:, :128], gain[0:1], half)
        key = head_norm(qkv[:, 128:256], gain[1:2], half)
        kv = jnp.concatenate([key, qkv[:, 256:].astype(BF16)], axis=1)
        for i in range(4):
            place = core if i < 2 else 1 - core
            row = pl.multiple_of(low * 512 + i % 2 * 256 + place * 128, 128)
            q_s[pl.ds(row, 128)] = query[i * 128 : i * 128 + 128]
            kv_s[pl.ds(pl.multiple_of(row + WIN, WIN), 128)] = kv[i * 128 : i * 128 + 128]
    for b in range(8):
        att[lax.rem(core + b, 2), b // 2] = attend(
            q_s[b * 128 : b * 128 + 128],
            kv_s[b * 128 : b * 128 + 256],
            first[b : b + 1],
            count[b : b + 1],
            anchor + (b * 128 - WIN),
        )
    keep[...] = att[0]
    give[...] = att[1]


def project_kernel(at, keep, got, weight, other, mine, away):
    y = at[0]
    rows = jnp.concatenate(
        [keep[...].reshape(512, 128), got[...].reshape(512, 128)], axis=1
    )
    both = jnp.concatenate([weight[...], other[...]], axis=1)
    part = lax.dot_general(rows, both, NT, preferred_element_type=F32)
    for t in range(4):
        block = part[t * 128 : t * 128 + 128]

        @pl.when(y == t)
        def _():
            mine[...] = block

        @pl.when(y != t)
        def _():
            away[lax.rem(t + 3 - y, 4)] = block.astype(BF16)


def middle_kernel(tok, mine, a, b, c, gain, middle, normed):
    total = mine[...] + a[...].astype(F32) + b[...].astype(F32) + c[...].astype(F32)
    mid = (tok[...].astype(F32) + total).astype(BF16)
    middle[...] = mid
    normed[...] = layer_norm(mid.astype(F32), gain[...])


def hidden_share(rows, weight):
    hidden = jax.nn.gelu(
        jnp.dot(rows, weight[:, :512], preferred_element_type=F32), approximate=True
    ).astype(BF16)
    return lax.dot_general(hidden, weight[:, 512:], NT, preferred_element_type=F32)


def mlp_first_kernel(a, b, c, d, weight, out):
    rows = jnp.concatenate([a[...], b[...], c[...], d[...]], axis=0)
    out[...] = hidden_share(rows, weight)


def mlp_second_kernel(rows, weight, part, out, *, at):
    total = part[at * 128 : at * 128 + 128] + hidden_share(rows[...], weight)
    out[...] = total.astype(out.dtype)


def mlp_second(rows, weight, part, at):
    return call(
        functools.partial(mlp_second_kernel, at=at),
        [((128, 1024), F32 if at == 0 else BF16)],
        [VMEM] * 3,
        "mlp_second",
    )(rows, weight, part)[0]


def end_kernel(middle, mine, a, b, c, out):
    total = middle[...].astype(F32) + mine[...]
    total += a[...].astype(F32) + b[...].astype(F32) + c[...].astype(F32)
    out[...] = total.astype(BF16)


def call(kernel, outs, specs, name, mib=8, scratch=(), flops=2**20, **more):
    return pl.pallas_call(
        kernel,
        out_shape=[jax.ShapeDtypeStruct(s, d) for s, d in outs],
        in_specs=specs,
        out_specs=[VMEM] * len(outs),
        scratch_shapes=list(scratch),
        compiler_params=params(mib),
        cost_estimate=pl.CostEstimate(flops=flops, bytes_accessed=2**21, transcendentals=0),
        name=name,
        **more,
    )


def fetch(value, axis, step):
    n = lax.axis_size(axis)
    return lax.ppermute(value, axis, [((i + step) % n, i) for i in range(n)])


def relay(block):
    half = block.shape[2] // 2
    right, left = fetch(block, "x", 1), fetch(block, "x", 3)
    far_low, far_high = fetch(right[:, :, :half], "x", 1), fetch(left[:, :, half:], "x", 3)
    return block, right, far_low, far_high, left


def local(
    tokens,
    win_first,
    win_count,
    norm1_gain,
    qkv_weight,
    qk_gain,
    out_weight,
    norm2_gain,
    up_weight,
    down_weight,
):
    y, core = lax.axis_index("y"), lax.axis_index("core")
    seq = lax.axis_index("z") * lax.axis_size("x") + lax.axis_index("x")
    at = jnp.stack([y, core, lax.axis_index("x"), seq * 1024]).astype(jnp.int32)
    first, count = win_first.reshape(8, 128), win_count.reshape(8, 128)

    (front,) = from_hbm(
        pack_kernel,
        [((8, 32, 512), BF16)],
        [jnp.transpose(qkv_weight, (1, 0, 2)), out_weight.T],
        "pack",
    )
    (normed,) = from_hbm(
        norm_kernel,
        [((128, 1024), BF16)],
        [tokens, norm1_gain.reshape(1, 1024)],
        "norm",
    )
    (back,) = from_hbm(
        mlp_pack_kernel,
        [((8, 32, 1024), BF16)],
        [up_weight, down_weight.T],
        "mlp_pack",
    )
    front = lax.all_to_all(front, "z", 0, 0, tiled=True)
    far = {k: fetch(normed, "y", k) for k in (1, 3, 2)}
    back, front = lax.optimization_barrier((back, front))
    weights = relay(front)
    back = lax.all_to_all(back, "z", 0, 0, tiled=True)
    far, _ = lax.optimization_barrier((far, (weights[1], weights[4])))
    own_low, own_high, border = call(
        collect_kernel,
        [((2, 128, 1024), BF16), ((2, 128, 1024), BF16), ((WIN, 1024), BF16)],
        [SMEM] + [VMEM] * 4,
        "collect",
    )(at, normed, far[1], far[2], far[3])
    peer_low, peer_high = fetch(own_low, "core", 1), fetch(own_high, "core", 1)
    spot = lambda z, x, y, core: ((z * 4 + x) * 4 + y) * 2 + core
    shift = lambda s, by: divmod((s + by) % 32, 4)
    near_own = lax.ppermute(
        border,
        ("z", "x", "y", "core"),
        [
            (spot(*divmod(s, 4), j, c), spot(*shift(s, 2 * c - 1), j, c))
            for s in range(32)
            for j in range(4)
            for c in range(2)
        ],
    )
    near_peer = fetch(near_own, "core", 1)
    keep, give, weight = call(
        attention_kernel,
        [((4, 128, 128), BF16), ((4, 128, 128), BF16), ((1024, 128), BF16)],
        [SMEM] + [VMEM] * 14,
        "attention",
        scratch=[
            pltpu.VMEM((1024, 512), BF16),
            pltpu.VMEM((1024, 128), BF16),
            pltpu.VMEM((1024 + 2 * WIN, 256), BF16),
            pltpu.VMEM((2, 4, 128, 128), BF16),
        ],
    )(at, own_low, own_high, peer_low, peer_high, *weights, near_own, near_peer, qk_gain, first, count)

    mlp_weights = relay(back)
    out_peer = fetch(weight, "core", 1)
    got = fetch(give, "core", 1)
    mine_attended, away = call(
        project_kernel,
        [((128, 1024), F32), ((3, 128, 1024), BF16)],
        [SMEM] + [VMEM] * 4,
        "project",
    )(at, keep, got, weight, out_peer)
    parts = [fetch(away[k - 1], "y", 4 - k) for k in (1, 3, 2)]
    middle, normed_two = call(
        middle_kernel,
        [((128, 1024), BF16)] * 2,
        [VMEM] * 6,
        "middle",
    )(tokens, mine_attended, *parts, norm2_gain.reshape(1, 1024))

    far = {k: fetch(normed_two, "y", k) for k in (1, 3, 2)}
    laid, far = lax.optimization_barrier((mlp_weights, far))
    (mlp_own,) = call(lay_kernel, [((1024, 1024), BF16)], [SMEM] + [VMEM] * 5, "mlp_lay")(
        at, *laid
    )
    mlp_peer = fetch(mlp_own, "core", 1)
    (part,) = call(mlp_first_kernel, [((512, 1024), F32)], [VMEM] * 5, "mlp_first", mib=16)(
        normed_two, far[1], far[2], far[3], mlp_own
    )
    parts = [fetch(mlp_second(far[k], mlp_peer, part, k), "y", 4 - k) for k in (1, 3, 2)]
    mine = mlp_second(normed_two, mlp_peer, part, 0)
    (out,) = call(end_kernel, [((128, 1024), BF16)], [VMEM] * 5, "end")(middle, mine, *parts)
    return out


def solution(mesh):
    fine = Mesh(mesh.devices.reshape(8, 4, 4, 2), ("z", "x", "y", "core"))
    seq, head = ("z", "x"), ("y", "core")
    return jax.shard_map(
        local,
        mesh=fine,
        in_specs=(
            P(seq + head, None),
            P(seq),
            P(seq),
            P(),
            P(seq, None, head),
            P(None, head, None),
            P(head, seq),
            P(),
            P(seq, head),
            P(head, seq),
        ),
        out_specs=P(seq + head, None),
        check_vma=False,
    )
```

```python
import jax
import jax.numpy as jnp
from jax import lax
from jax.experimental import pallas as pl
from jax.experimental.pallas import tpu as pltpu
from jax.sharding import Mesh, PartitionSpec as P

WIN = 64
F32, BF16 = jnp.float32, jnp.bfloat16
NT = (((1,), (1,)), ((), ()))
VMEM = pl.BlockSpec(memory_space=pltpu.VMEM)
HBM = pl.BlockSpec(memory_space=pltpu.HBM)
SMEM = pl.BlockSpec(memory_space=pltpu.SMEM)


def params(mib):
    return pltpu.CompilerParams(vmem_limit_bytes=mib * 2**20)


def layer_norm(values, gain):
    center = values - jnp.mean(values, axis=-1, keepdims=True)
    spread = jnp.mean(center * center, axis=-1, keepdims=True)
    return (center * lax.rsqrt(spread + 1e-06) * gain).astype(BF16)


def head_norm(values, gain, half):
    square = values * values
    low = jnp.sum(jnp.where(half, square, 0.0), axis=-1, keepdims=True)
    high = jnp.sum(jnp.where(half, 0.0, square), axis=-1, keepdims=True)
    scale = lax.rsqrt(jnp.where(half, low, high) * (1.0 / 64) + 1e-06)
    return (values * scale * gain).astype(BF16)


def first_half(rows):
    return lax.broadcasted_iota(jnp.int32, (rows, 128), 1) < 64


def bring(held, here, sems):
    copies = [
        pltpu.make_async_copy(a, b, sems.at[i]) for i, (a, b) in enumerate(zip(held, here))
    ]
    for copy in copies:
        copy.start()
    return copies


def pack_kernel(*refs):
    held, front, here, sems = refs[:2], refs[2], refs[3:5], refs[5]
    for copy in bring(held, here, sems):
        copy.wait()
    qkv, out_t = here
    pack = jnp.concatenate([qkv[0], qkv[1], qkv[2], out_t[...]], axis=1)
    for i in range(8):
        front[i] = pack


def norm_kernel(*refs):
    held, normed, here, sems = refs[:2], refs[2], refs[3:5], refs[5]
    for copy in bring(held, here, sems):
        copy.wait()
    tok, gain = here
    normed[...] = layer_norm(tok[...].astype(F32), gain[...])


def mlp_pack_kernel(*refs):
    held, back, here, sems = refs[:2], refs[2], refs[3:5], refs[5]
    for copy in bring(held, here, sems):
        copy.wait()
    up, down_t = here
    pack = jnp.concatenate([up[...], down_t[...]], axis=1)
    for i in range(8):
        back[i] = pack


def from_hbm(kernel, outs, given, name):
    return call(
        kernel,
        outs,
        [HBM] * len(given),
        name,
        scratch=[pltpu.VMEM(v.shape, v.dtype) for v in given]
        + [pltpu.SemaphoreType.DMA((len(given),))],
    )(*[pltpu.with_memory_space_constraint(v, pltpu.HBM) for v in given])


def collect_kernel(at, *refs):
    blocks, own, border = refs[:4], refs[4:6], refs[6]
    y, core = at[0], at[1]
    for k in range(4):
        t = lax.rem(y + k, 4)
        for low in range(2):

            @pl.when(t // 2 == low)
            def _():
                own[low][lax.rem(t, 2)] = blocks[k][...]

        @pl.when((core == 0) & (t == 0))
        def _():
            border[...] = blocks[k][:WIN]

        @pl.when((core == 1) & (t == 3))
        def _():
            border[...] = blocks[k][128 - WIN :]


def lay(x, here, right, far_low, far_high, left, out):
    half = out.shape[1] // 2
    for k, block in enumerate((here, right, None, left)):
        base = lax.rem(x + k, 4) * 32
        for z in range(8):
            rows = pl.ds(pl.multiple_of(z * 128 + base, 32), 32)
            if block is None:
                out[rows, :half] = far_low[z]
                out[rows, half:] = far_high[z]
            else:
                out[rows] = block[z]


def lay_kernel(at, *refs):
    lay(at[2], *refs)


def attend(query, kv, first, count, key_start):
    lower = jnp.broadcast_to(first, (128, 128)).T
    upper = lower + jnp.broadcast_to(count, (128, 128)).T
    index = key_start + lax.broadcasted_iota(jnp.int32, (128, 256), 1)
    lower = jnp.concatenate([lower, lower], axis=1)
    upper = jnp.concatenate([upper, upper], axis=1)
    allowed = (index >= lower) & (index < upper)
    low = first_half(128)
    values = kv[:, 128:]
    one, none = jnp.ones_like(values), jnp.zeros_like(query)
    pick = first_half(256)
    sums = []
    for h in range(2):
        own = low if h == 0 else ~low
        score = lax.dot_general(
            jnp.where(own, query, none), kv[:, :128], NT, preferred_element_type=F32
        )
        weight = jnp.where(allowed, jnp.exp(score * 0.125), 0.0).astype(BF16)
        held = jnp.where(pick if h == 0 else ~pick, values, one)
        sums.append(jnp.dot(weight, held, preferred_element_type=F32))
    mixed = jnp.where(low, sums[0], sums[1])
    total = pltpu.roll(jnp.where(low, sums[1], sums[0]), 64, 1)
    return (mixed / total).astype(BF16)


def attention_kernel(
    at, own_low, own_high, peer_low, peer_high, here, right, far_low, far_high, left,
    near_own, near_peer, gains, first, count, keep, both, weight, q_s, kv_s, att,
):
    lay(at[2], here, right, far_low, far_high, left, weight)
    core, anchor = at[1], at[3]
    gain = gains[...]
    gain = jnp.concatenate([gain[:, 0], gain[:, 1]], axis=1)

    rows = jnp.concatenate([near_own[...], near_peer[...]], axis=0)
    part = jnp.dot(rows, weight[:, 128:384], preferred_element_type=F32)
    key = head_norm(part[:, :128], gain[1:2], first_half(2 * WIN))
    kv = jnp.concatenate([key, part[:, 128:].astype(BF16)], axis=1)
    end = WIN + 1024
    kv_s[pl.ds(pl.multiple_of((1 - core) * end, WIN), WIN)] = kv[:WIN]
    kv_s[pl.ds(pl.multiple_of(core * end, WIN), WIN)] = kv[WIN:]

    half = first_half(512)
    for low, (own, peer) in enumerate(((own_low, peer_low), (own_high, peer_high))):
        rows = jnp.concatenate([own[0], own[1], peer[0], peer[1]], axis=0)
        qkv = jnp.dot(rows, weight[:, :384], preferred_element_type=F32)
        query = head_norm(qkv[:, :128], gain[0:1], half)
        key = head_norm(qkv[:, 128:256], gain[1:2], half)
        kv = jnp.concatenate([key, qkv[:, 256:].astype(BF16)], axis=1)
        for i in range(4):
            place = core if i < 2 else 1 - core
            row = pl.multiple_of(low * 512 + i % 2 * 256 + place * 128, 128)
            q_s[pl.ds(row, 128)] = query[i * 128 : i * 128 + 128]
            kv_s[pl.ds(pl.multiple_of(row + WIN, WIN), 128)] = kv[i * 128 : i * 128 + 128]
    for b in range(8):
        att[lax.rem(core + b, 2), b // 2] = attend(
            q_s[b * 128 : b * 128 + 128],
            kv_s[b * 128 : b * 128 + 256],
            first[b : b + 1],
            count[b : b + 1],
            anchor + (b * 128 - WIN),
        )
    keep[...] = att[0].reshape(512, 128)
    both[:512] = att[1].reshape(512, 128)
    both[512:] = weight[:, 384:]


def project_kernel(at, keep, sent, got, mine, away):
    y = at[0]
    rows = jnp.concatenate([keep[...], got[:512]], axis=1)
    weight = jnp.concatenate([sent[512:], got[512:]], axis=1)
    part = lax.dot_general(rows, weight, NT, preferred_element_type=F32)
    for t in range(4):
        block = part[t * 128 : t * 128 + 128]

        @pl.when(y == t)
        def _():
            mine[...] = block

        @pl.when(y != t)
        def _():
            away[lax.rem(t + 3 - y, 4)] = block.astype(BF16)


def middle_kernel(tok, mine, a, b, c, gain, middle, normed):
    total = mine[...] + a[...].astype(F32) + b[...].astype(F32) + c[...].astype(F32)
    mid = (tok[...].astype(F32) + total).astype(BF16)
    middle[...] = mid
    normed[...] = layer_norm(mid.astype(F32), gain[...])


def hidden_share(rows, weight):
    hidden = jax.nn.gelu(
        jnp.dot(rows, weight[:, :512], preferred_element_type=F32), approximate=True
    ).astype(BF16)
    return lax.dot_general(hidden, weight[:, 512:], NT, preferred_element_type=F32)


def mlp_first_kernel(a, b, c, d, weight, out):
    rows = jnp.concatenate([a[...], b[...], c[...], d[...]], axis=0)
    out[...] = hidden_share(rows, weight)


def mlp_second_kernel(a, b, c, d, weight, part, mine, to_b, to_c, to_d):
    rows = jnp.concatenate([a[...], b[...], c[...], d[...]], axis=0)
    total = part[...] + hidden_share(rows, weight)
    mine[...] = total[:128]
    for i, out in enumerate((to_b, to_c, to_d)):
        out[...] = total[i * 128 + 128 : i * 128 + 256].astype(BF16)


def end_kernel(middle, mine, a, b, c, out):
    total = middle[...].astype(F32) + mine[...]
    total += a[...].astype(F32) + b[...].astype(F32) + c[...].astype(F32)
    out[...] = total.astype(BF16)


def call(kernel, outs, specs, name, mib=8, scratch=(), flops=2**20, **more):
    return pl.pallas_call(
        kernel,
        out_shape=[jax.ShapeDtypeStruct(s, d) for s, d in outs],
        in_specs=specs,
        out_specs=[VMEM] * len(outs),
        scratch_shapes=list(scratch),
        compiler_params=params(mib),
        cost_estimate=pl.CostEstimate(flops=flops, bytes_accessed=2**21, transcendentals=0),
        name=name,
        **more,
    )


def fetch(value, axis, step):
    n = lax.axis_size(axis)
    return lax.ppermute(value, axis, [((i + step) % n, i) for i in range(n)])


def relay(block):
    half = block.shape[2] // 2
    right, left = fetch(block, "x", 1), fetch(block, "x", 3)
    far_low, far_high = fetch(right[:, :, :half], "x", 1), fetch(left[:, :, half:], "x", 3)
    return block, right, far_low, far_high, left


def local(
    tokens,
    win_first,
    win_count,
    norm1_gain,
    qkv_weight,
    qk_gain,
    out_weight,
    norm2_gain,
    up_weight,
    down_weight,
):
    y, core = lax.axis_index("y"), lax.axis_index("core")
    seq = lax.axis_index("z") * lax.axis_size("x") + lax.axis_index("x")
    at = jnp.stack([y, core, lax.axis_index("x"), seq * 1024]).astype(jnp.int32)
    first, count = win_first.reshape(8, 128), win_count.reshape(8, 128)

    (front,) = from_hbm(
        pack_kernel,
        [((8, 32, 512), BF16)],
        [jnp.transpose(qkv_weight, (1, 0, 2)), out_weight.T],
        "pack",
    )
    (normed,) = from_hbm(
        norm_kernel,
        [((128, 1024), BF16)],
        [tokens, norm1_gain.reshape(1, 1024)],
        "norm",
    )
    (back,) = from_hbm(
        mlp_pack_kernel,
        [((8, 32, 1024), BF16)],
        [up_weight, down_weight.T],
        "mlp_pack",
    )
    front = lax.all_to_all(front, "z", 0, 0, tiled=True)
    far = {k: fetch(normed, "y", k) for k in (1, 3, 2)}
    back, front = lax.optimization_barrier((back, front))
    weights = relay(front)
    back = lax.all_to_all(back, "z", 0, 0, tiled=True)
    far, _ = lax.optimization_barrier((far, (weights[1], weights[4])))
    own_low, own_high, border = call(
        collect_kernel,
        [((2, 128, 1024), BF16), ((2, 128, 1024), BF16), ((WIN, 1024), BF16)],
        [SMEM] + [VMEM] * 4,
        "collect",
    )(at, normed, far[1], far[2], far[3])
    peer_low, peer_high = fetch(own_low, "core", 1), fetch(own_high, "core", 1)
    spot = lambda z, x, y, core: ((z * 4 + x) * 4 + y) * 2 + core
    shift = lambda s, by: divmod((s + by) % 32, 4)
    near_own = lax.ppermute(
        border,
        ("z", "x", "y", "core"),
        [
            (spot(*divmod(s, 4), j, c), spot(*shift(s, 2 * c - 1), j, c))
            for s in range(32)
            for j in range(4)
            for c in range(2)
        ],
    )
    near_peer = fetch(near_own, "core", 1)
    keep, both = call(
        attention_kernel,
        [((512, 128), BF16), ((1536, 128), BF16)],
        [SMEM] + [VMEM] * 14,
        "attention",
        scratch=[
            pltpu.VMEM((1024, 512), BF16),
            pltpu.VMEM((1024, 128), BF16),
            pltpu.VMEM((1024 + 2 * WIN, 256), BF16),
            pltpu.VMEM((2, 4, 128, 128), BF16),
        ],
    )(at, own_low, own_high, peer_low, peer_high, *weights, near_own, near_peer, qk_gain, first, count)

    mlp_weights = relay(back)
    got = fetch(both, "core", 1)
    mine_attended, away = call(
        project_kernel,
        [((128, 1024), F32), ((3, 128, 1024), BF16)],
        [SMEM] + [VMEM] * 3,
        "project",
    )(at, keep, both, got)
    parts = [fetch(away[k - 1], "y", 4 - k) for k in (1, 3, 2)]
    middle, normed_two = call(
        middle_kernel,
        [((128, 1024), BF16)] * 2,
        [VMEM] * 6,
        "middle",
    )(tokens, mine_attended, *parts, norm2_gain.reshape(1, 1024))

    far = {k: fetch(normed_two, "y", k) for k in (1, 3, 2)}
    laid, far = lax.optimization_barrier((mlp_weights, far))
    (mlp_own,) = call(lay_kernel, [((1024, 1024), BF16)], [SMEM] + [VMEM] * 5, "mlp_lay")(
        at, *laid
    )
    mlp_peer = fetch(mlp_own, "core", 1)
    (part,) = call(mlp_first_kernel, [((512, 1024), F32)], [VMEM] * 5, "mlp_first", mib=16)(
        normed_two, far[1], far[2], far[3], mlp_own
    )
    mine, *away = call(
        mlp_second_kernel,
        [((128, 1024), F32)] + [((128, 1024), BF16)] * 3,
        [VMEM] * 6,
        "mlp_second",
        mib=16,
    )(normed_two, far[1], far[2], far[3], mlp_peer, part)
    parts = [fetch(away[k - 1], "y", 4 - k) for k in (1, 3, 2)]
    (out,) = call(end_kernel, [((128, 1024), BF16)], [VMEM] * 5, "end")(middle, mine, *parts)
    return out


def solution(mesh):
    fine = Mesh(mesh.devices.reshape(8, 4, 4, 2), ("z", "x", "y", "core"))
    seq, head = ("z", "x"), ("y", "core")
    return jax.shard_map(
        local,
        mesh=fine,
        in_specs=(
            P(seq + head, None),
            P(seq),
            P(seq),
            P(),
            P(seq, None, head),
            P(None, head, None),
            P(head, seq),
            P(),
            P(seq, head),
            P(head, seq),
        ),
        out_specs=P(seq + head, None),
        check_vma=False,
    )
```

```python
import jax
import jax.numpy as jnp
from jax import lax
from jax.experimental import pallas as pl
from jax.experimental.pallas import tpu as pltpu
from jax.sharding import Mesh, PartitionSpec as P

WIN = 64
F32, BF16 = jnp.float32, jnp.bfloat16
NT = (((1,), (1,)), ((), ()))
VMEM = pl.BlockSpec(memory_space=pltpu.VMEM)
HBM = pl.BlockSpec(memory_space=pltpu.HBM)
SMEM = pl.BlockSpec(memory_space=pltpu.SMEM)


def params(mib):
    return pltpu.CompilerParams(vmem_limit_bytes=mib * 2**20)


def layer_norm(values, gain):
    center = values - jnp.mean(values, axis=-1, keepdims=True)
    spread = jnp.mean(center * center, axis=-1, keepdims=True)
    return (center * lax.rsqrt(spread + 1e-06) * gain).astype(BF16)


def head_norm(values, gain, half):
    square = values * values
    low = jnp.sum(jnp.where(half, square, 0.0), axis=-1, keepdims=True)
    high = jnp.sum(jnp.where(half, 0.0, square), axis=-1, keepdims=True)
    scale = lax.rsqrt(jnp.where(half, low, high) * (1.0 / 64) + 1e-06)
    return (values * scale * gain).astype(BF16)


def first_half(rows):
    return lax.broadcasted_iota(jnp.int32, (rows, 128), 1) < 64


def bring(held, here, sems):
    copies = [
        pltpu.make_async_copy(a, b, sems.at[i]) for i, (a, b) in enumerate(zip(held, here))
    ]
    for copy in copies:
        copy.start()
    return copies


def pack_kernel(*refs):
    held, front, here, sems = refs[:2], refs[2], refs[3:5], refs[5]
    for copy in bring(held, here, sems):
        copy.wait()
    qkv, out_t = here
    pack = jnp.concatenate([qkv[0], qkv[1], qkv[2], out_t[...]], axis=1)
    for i in range(8):
        front[i] = pack


def norm_kernel(*refs):
    held, normed, here, sems = refs[:2], refs[2], refs[3:5], refs[5]
    for copy in bring(held, here, sems):
        copy.wait()
    tok, gain = here
    normed[...] = layer_norm(tok[...].astype(F32), gain[...])


def mlp_pack_kernel(*refs):
    held, back, here, sems = refs[:2], refs[2], refs[3:5], refs[5]
    for copy in bring(held, here, sems):
        copy.wait()
    up, down_t = here
    pack = jnp.concatenate([up[...], down_t[...]], axis=1)
    for i in range(8):
        back[i] = pack


def from_hbm(kernel, outs, given, name):
    return call(
        kernel,
        outs,
        [HBM] * len(given),
        name,
        scratch=[pltpu.VMEM(v.shape, v.dtype) for v in given]
        + [pltpu.SemaphoreType.DMA((len(given),))],
    )(*[pltpu.with_memory_space_constraint(v, pltpu.HBM) for v in given])


def collect_kernel(at, *refs):
    blocks, own, border = refs[:4], refs[4:6], refs[6]
    y, core = at[0], at[1]
    for k in range(4):
        t = lax.rem(y + k, 4)
        for low in range(2):

            @pl.when(t // 2 == low)
            def _():
                own[low][lax.rem(t, 2)] = blocks[k][...]

        @pl.when((core == 0) & (t == 0))
        def _():
            border[...] = blocks[k][:WIN]

        @pl.when((core == 1) & (t == 3))
        def _():
            border[...] = blocks[k][128 - WIN :]


def lay(x, here, right, far_low, far_high, left, out):
    half = out.shape[1] // 2
    for k, block in enumerate((here, right, None, left)):
        base = lax.rem(x + k, 4) * 32
        for z in range(8):
            rows = pl.ds(pl.multiple_of(z * 128 + base, 32), 32)
            if block is None:
                out[rows, :half] = far_low[z]
                out[rows, half:] = far_high[z]
            else:
                out[rows] = block[z]


def lay_kernel(at, *refs):
    lay(at[2], *refs)


def attend(query, kv, first, count, key_start):
    lower = jnp.broadcast_to(first, (128, 128)).T
    upper = lower + jnp.broadcast_to(count, (128, 128)).T
    index = key_start + lax.broadcasted_iota(jnp.int32, (128, 256), 1)
    lower = jnp.concatenate([lower, lower], axis=1)
    upper = jnp.concatenate([upper, upper], axis=1)
    allowed = (index >= lower) & (index < upper)
    low = first_half(128)
    values = kv[:, 128:]
    one, none = jnp.ones_like(values), jnp.zeros_like(query)
    pick = first_half(256)
    sums = []
    for h in range(2):
        own = low if h == 0 else ~low
        score = lax.dot_general(
            jnp.where(own, query, none), kv[:, :128], NT, preferred_element_type=F32
        )
        weight = jnp.where(allowed, jnp.exp(score * 0.125), 0.0).astype(BF16)
        held = jnp.where(pick if h == 0 else ~pick, values, one)
        sums.append(jnp.dot(weight, held, preferred_element_type=F32))
    mixed = jnp.where(low, sums[0], sums[1])
    total = pltpu.roll(jnp.where(low, sums[1], sums[0]), 64, 1)
    return (mixed / total).astype(BF16)


def attention_kernel(
    at, own_low, own_high, peer_low, peer_high, here, right, far_low, far_high, left,
    near_own, near_peer, gains, first, count, keep, both, weight, q_s, kv_s, att,
):
    lay(at[2], here, right, far_low, far_high, left, weight)
    core, anchor = at[1], at[3]
    gain = gains[...]
    gain = jnp.concatenate([gain[:, 0], gain[:, 1]], axis=1)

    rows = jnp.concatenate([near_own[...], near_peer[...]], axis=0)
    part = jnp.dot(rows, weight[:, 128:384], preferred_element_type=F32)
    key = head_norm(part[:, :128], gain[1:2], first_half(2 * WIN))
    kv = jnp.concatenate([key, part[:, 128:].astype(BF16)], axis=1)
    end = WIN + 1024
    kv_s[pl.ds(pl.multiple_of((1 - core) * end, WIN), WIN)] = kv[:WIN]
    kv_s[pl.ds(pl.multiple_of(core * end, WIN), WIN)] = kv[WIN:]

    half = first_half(512)
    for low, (own, peer) in enumerate(((own_low, peer_low), (own_high, peer_high))):
        rows = jnp.concatenate([own[0], own[1], peer[0], peer[1]], axis=0)
        qkv = jnp.dot(rows, weight[:, :384], preferred_element_type=F32)
        query = head_norm(qkv[:, :128], gain[0:1], half)
        key = head_norm(qkv[:, 128:256], gain[1:2], half)
        kv = jnp.concatenate([key, qkv[:, 256:].astype(BF16)], axis=1)
        for i in range(4):
            place = core if i < 2 else 1 - core
            row = pl.multiple_of(low * 512 + i % 2 * 256 + place * 128, 128)
            q_s[pl.ds(row, 128)] = query[i * 128 : i * 128 + 128]
            kv_s[pl.ds(pl.multiple_of(row + WIN, WIN), 128)] = kv[i * 128 : i * 128 + 128]
    for b in range(8):
        att[lax.rem(core + b, 2), b // 2] = attend(
            q_s[b * 128 : b * 128 + 128],
            kv_s[b * 128 : b * 128 + 256],
            first[b : b + 1],
            count[b : b + 1],
            anchor + (b * 128 - WIN),
        )
    keep[...] = att[0].reshape(512, 128)
    both[:512] = att[1].reshape(512, 128)
    both[512:] = weight[:, 384:]


def project_kernel(at, keep, sent, got, mine, away):
    y = at[0]
    rows = jnp.concatenate([keep[...], got[:512]], axis=1)
    weight = jnp.concatenate([sent[512:], got[512:]], axis=1)
    part = lax.dot_general(rows, weight, NT, preferred_element_type=F32)
    for t in range(4):
        block = part[t * 128 : t * 128 + 128]

        @pl.when(y == t)
        def _():
            mine[...] = block

        @pl.when(y != t)
        def _():
            away[lax.rem(t + 3 - y, 4)] = block.astype(BF16)


def middle_kernel(tok, mine, a, b, c, gain, middle, normed):
    total = mine[...] + a[...].astype(F32) + b[...].astype(F32) + c[...].astype(F32)
    mid = (tok[...].astype(F32) + total).astype(BF16)
    middle[...] = mid
    normed[...] = layer_norm(mid.astype(F32), gain[...])


def hidden_share(rows, weight):
    hidden = jax.nn.gelu(
        jnp.dot(rows, weight[:, :512], preferred_element_type=F32), approximate=True
    ).astype(BF16)
    return lax.dot_general(hidden, weight[:, 512:], NT, preferred_element_type=F32)


def mlp_first_kernel(a, b, c, d, weight, out):
    rows = jnp.concatenate([a[...], b[...], c[...], d[...]], axis=0)
    out[...] = hidden_share(rows, weight)


def mlp_second_kernel(a, b, c, d, weight, part, mine, to_b, to_c, to_d):
    rows = jnp.concatenate([a[...], b[...], c[...], d[...]], axis=0)
    total = part[...] + hidden_share(rows, weight)
    mine[...] = total[:128]
    for i, out in enumerate((to_b, to_c, to_d)):
        out[...] = total[i * 128 + 128 : i * 128 + 256].astype(BF16)


def end_kernel(middle, mine, a, b, c, out):
    total = middle[...].astype(F32) + mine[...]
    total += a[...].astype(F32) + b[...].astype(F32) + c[...].astype(F32)
    out[...] = total.astype(BF16)


def call(kernel, outs, specs, name, mib=8, scratch=(), flops=2**20, **more):
    return pl.pallas_call(
        kernel,
        out_shape=[jax.ShapeDtypeStruct(s, d) for s, d in outs],
        in_specs=specs,
        out_specs=[VMEM] * len(outs),
        scratch_shapes=list(scratch),
        compiler_params=params(mib),
        cost_estimate=pl.CostEstimate(flops=flops, bytes_accessed=2**21, transcendentals=0),
        name=name,
        **more,
    )


def fetch(value, axis, step):
    n = lax.axis_size(axis)
    return lax.ppermute(value, axis, [((i + step) % n, i) for i in range(n)])


def relay(block):
    half = block.shape[2] // 2
    right, left = fetch(block, "x", 1), fetch(block, "x", 3)
    far_low, far_high = fetch(right[:, :, :half], "x", 1), fetch(left[:, :, half:], "x", 3)
    return block, right, far_low, far_high, left


def local(
    tokens,
    win_first,
    win_count,
    norm1_gain,
    qkv_weight,
    qk_gain,
    out_weight,
    norm2_gain,
    up_weight,
    down_weight,
):
    y, core = lax.axis_index("y"), lax.axis_index("core")
    seq = lax.axis_index("z") * lax.axis_size("x") + lax.axis_index("x")
    at = jnp.stack([y, core, lax.axis_index("x"), seq * 1024]).astype(jnp.int32)
    first, count = win_first.reshape(8, 128), win_count.reshape(8, 128)

    (front,) = from_hbm(
        pack_kernel,
        [((8, 32, 512), BF16)],
        [jnp.transpose(qkv_weight, (1, 0, 2)), out_weight.T],
        "pack",
    )
    (normed,) = from_hbm(
        norm_kernel,
        [((128, 1024), BF16)],
        [tokens, norm1_gain.reshape(1, 1024)],
        "norm",
    )
    (back,) = from_hbm(
        mlp_pack_kernel,
        [((8, 32, 1024), BF16)],
        [up_weight, down_weight.T],
        "mlp_pack",
    )
    front = lax.all_to_all(front, "z", 0, 0, tiled=True)
    far = {k: fetch(normed, "y", k) for k in (1, 3, 2)}
    back, front = lax.optimization_barrier((back, front))
    weights = relay(front)
    back = lax.all_to_all(back, "z", 0, 0, tiled=True)
    far, _ = lax.optimization_barrier((far, (weights[1], weights[4])))
    own_low, own_high, border = call(
        collect_kernel,
        [((2, 128, 1024), BF16), ((2, 128, 1024), BF16), ((WIN, 1024), BF16)],
        [SMEM] + [VMEM] * 4,
        "collect",
    )(at, normed, far[1], far[2], far[3])
    peer_low, peer_high = fetch(own_low, "core", 1), fetch(own_high, "core", 1)
    spot = lambda z, x, y, core: ((z * 4 + x) * 4 + y) * 2 + core
    shift = lambda s, by: divmod((s + by) % 32, 4)
    near_own = lax.ppermute(
        border,
        ("z", "x", "y", "core"),
        [
            (spot(*divmod(s, 4), j, c), spot(*shift(s, 2 * c - 1), j, c))
            for s in range(32)
            for j in range(4)
            for c in range(2)
        ],
    )
    near_peer = fetch(near_own, "core", 1)
    keep, both = call(
        attention_kernel,
        [((512, 128), BF16), ((1536, 128), BF16)],
        [SMEM] + [VMEM] * 14,
        "attention",
        scratch=[
            pltpu.VMEM((1024, 512), BF16),
            pltpu.VMEM((1024, 128), BF16),
            pltpu.VMEM((1024 + 2 * WIN, 256), BF16),
            pltpu.VMEM((2, 4, 128, 128), BF16),
        ],
    )(at, own_low, own_high, peer_low, peer_high, *weights, near_own, near_peer, qk_gain, first, count)

    mlp_weights = relay(back)
    got = fetch(both, "core", 1)
    mine_attended, away = call(
        project_kernel,
        [((128, 1024), F32), ((3, 128, 1024), BF16)],
        [SMEM] + [VMEM] * 3,
        "project",
    )(at, keep, both, got)
    parts = [fetch(away[k - 1], "y", 4 - k) for k in (1, 3, 2)]
    middle, normed_two = call(
        middle_kernel,
        [((128, 1024), BF16)] * 2,
        [VMEM] * 6,
        "middle",
    )(tokens, mine_attended, *parts, norm2_gain.reshape(1, 1024))

    far = {k: fetch(normed_two, "y", k) for k in (1, 3, 2)}
    (mlp_own,) = call(lay_kernel, [((1024, 1024), BF16)], [SMEM] + [VMEM] * 5, "mlp_lay")(
        at, *mlp_weights
    )
    mlp_own, far = lax.optimization_barrier((mlp_own, far))
    mlp_peer = fetch(mlp_own, "core", 1)
    (part,) = call(mlp_first_kernel, [((512, 1024), F32)], [VMEM] * 5, "mlp_first", mib=16)(
        normed_two, far[1], far[2], far[3], mlp_own
    )
    mine, *away = call(
        mlp_second_kernel,
        [((128, 1024), F32)] + [((128, 1024), BF16)] * 3,
        [VMEM] * 6,
        "mlp_second",
        mib=16,
    )(normed_two, far[1], far[2], far[3], mlp_peer, part)
    parts = [fetch(away[k - 1], "y", 4 - k) for k in (1, 3, 2)]
    (out,) = call(end_kernel, [((128, 1024), BF16)], [VMEM] * 5, "end")(middle, mine, *parts)
    return out


def solution(mesh):
    fine = Mesh(mesh.devices.reshape(8, 4, 4, 2), ("z", "x", "y", "core"))
    seq, head = ("z", "x"), ("y", "core")
    return jax.shard_map(
        local,
        mesh=fine,
        in_specs=(
            P(seq + head, None),
            P(seq),
            P(seq),
            P(),
            P(seq, None, head),
            P(None, head, None),
            P(head, seq),
            P(),
            P(seq, head),
            P(head, seq),
        ),
        out_specs=P(seq + head, None),
        check_vma=False,
    )
```

```python
import jax
import jax.numpy as jnp
from jax import lax
from jax.experimental import pallas as pl
from jax.experimental.pallas import tpu as pltpu
from jax.sharding import Mesh, PartitionSpec as P

WIN = 64
F32, BF16 = jnp.float32, jnp.bfloat16
NT = (((1,), (1,)), ((), ()))
VMEM = pl.BlockSpec(memory_space=pltpu.VMEM)
HBM = pl.BlockSpec(memory_space=pltpu.HBM)
SMEM = pl.BlockSpec(memory_space=pltpu.SMEM)


def params(mib):
    return pltpu.CompilerParams(vmem_limit_bytes=mib * 2**20)


def layer_norm(values, gain):
    center = values - jnp.mean(values, axis=-1, keepdims=True)
    spread = jnp.mean(center * center, axis=-1, keepdims=True)
    return (center * lax.rsqrt(spread + 1e-06) * gain).astype(BF16)


def head_norm(values, gain, half):
    square = values * values
    low = jnp.sum(jnp.where(half, square, 0.0), axis=-1, keepdims=True)
    high = jnp.sum(jnp.where(half, 0.0, square), axis=-1, keepdims=True)
    scale = lax.rsqrt(jnp.where(half, low, high) * (1.0 / 64) + 1e-06)
    return (values * scale * gain).astype(BF16)


def first_half(rows):
    return lax.broadcasted_iota(jnp.int32, (rows, 128), 1) < 64


def bring(held, here, sems):
    copies = [
        pltpu.make_async_copy(a, b, sems.at[i]) for i, (a, b) in enumerate(zip(held, here))
    ]
    for copy in copies:
        copy.start()
    return copies


def pack_kernel(*refs):
    held, front, here, sems = refs[:2], refs[2], refs[3:5], refs[5]
    for copy in bring(held, here, sems):
        copy.wait()
    qkv, out_t = here
    pack = jnp.concatenate([qkv[0], qkv[1], qkv[2], out_t[...]], axis=1)
    for i in range(8):
        front[i] = pack


def norm_kernel(*refs):
    held, normed, here, sems = refs[:2], refs[2], refs[3:5], refs[5]
    for copy in bring(held, here, sems):
        copy.wait()
    tok, gain = here
    normed[...] = layer_norm(tok[...].astype(F32), gain[...])


def mlp_pack_kernel(*refs):
    held, back, here, sems = refs[:2], refs[2], refs[3:5], refs[5]
    for copy in bring(held, here, sems):
        copy.wait()
    up, down_t = here
    pack = jnp.concatenate([up[...], down_t[...]], axis=1)
    for i in range(8):
        back[i] = pack


def from_hbm(kernel, outs, given, name):
    return call(
        kernel,
        outs,
        [HBM] * len(given),
        name,
        scratch=[pltpu.VMEM(v.shape, v.dtype) for v in given]
        + [pltpu.SemaphoreType.DMA((len(given),))],
    )(*[pltpu.with_memory_space_constraint(v, pltpu.HBM) for v in given])


def collect_kernel(at, *refs):
    blocks, own, border = refs[:4], refs[4:6], refs[6]
    y, core = at[0], at[1]
    for k in range(4):
        t = lax.rem(y + k, 4)
        for low in range(2):

            @pl.when(t // 2 == low)
            def _():
                own[low][lax.rem(t, 2)] = blocks[k][...]

        @pl.when((core == 0) & (t == 0))
        def _():
            border[...] = blocks[k][:WIN]

        @pl.when((core == 1) & (t == 3))
        def _():
            border[...] = blocks[k][128 - WIN :]


def lay(x, here, right, far_low, far_high, left, out):
    half = out.shape[1] // 2
    for k, block in enumerate((here, right, None, left)):
        base = lax.rem(x + k, 4) * 32
        for z in range(8):
            rows = pl.ds(pl.multiple_of(z * 128 + base, 32), 32)
            if block is None:
                out[rows, :half] = far_low[z]
                out[rows, half:] = far_high[z]
            else:
                out[rows] = block[z]


def lay_kernel(at, *refs):
    lay(at[2], *refs)


def attend(query, kv, first, count, key_start):
    lower = jnp.broadcast_to(first, (128, 128)).T
    upper = lower + jnp.broadcast_to(count, (128, 128)).T
    index = key_start + lax.broadcasted_iota(jnp.int32, (128, 256), 1)
    lower = jnp.concatenate([lower, lower], axis=1)
    upper = jnp.concatenate([upper, upper], axis=1)
    allowed = (index >= lower) & (index < upper)
    low = first_half(128)
    values = kv[:, 128:]
    one, none = jnp.ones_like(values), jnp.zeros_like(query)
    pick = first_half(256)
    sums = []
    for h in range(2):
        own = low if h == 0 else ~low
        score = lax.dot_general(
            jnp.where(own, query, none), kv[:, :128], NT, preferred_element_type=F32
        )
        weight = jnp.where(allowed, jnp.exp(score * 0.125), 0.0).astype(BF16)
        held = jnp.where(pick if h == 0 else ~pick, values, one)
        sums.append(jnp.dot(weight, held, preferred_element_type=F32))
    mixed = jnp.where(low, sums[0], sums[1])
    total = pltpu.roll(jnp.where(low, sums[1], sums[0]), 64, 1)
    return (mixed / total).astype(BF16)


def attention_kernel(
    at, own_low, own_high, peer_low, peer_high, here, right, far_low, far_high, left,
    near_own, near_peer, gains, first, count, keep, both, weight, q_s, kv_s, att,
):
    lay(at[2], here, right, far_low, far_high, left, weight)
    core, anchor = at[1], at[3]
    gain = gains[...]
    gain = jnp.concatenate([gain[:, 0], gain[:, 1]], axis=1)

    rows = jnp.concatenate([near_own[...], near_peer[...]], axis=0)
    part = jnp.dot(rows, weight[:, 128:384], preferred_element_type=F32)
    key = head_norm(part[:, :128], gain[1:2], first_half(2 * WIN))
    kv = jnp.concatenate([key, part[:, 128:].astype(BF16)], axis=1)
    end = WIN + 1024
    kv_s[pl.ds(pl.multiple_of((1 - core) * end, WIN), WIN)] = kv[:WIN]
    kv_s[pl.ds(pl.multiple_of(core * end, WIN), WIN)] = kv[WIN:]

    half = first_half(512)
    for low, (own, peer) in enumerate(((own_low, peer_low), (own_high, peer_high))):
        rows = jnp.concatenate([own[0], own[1], peer[0], peer[1]], axis=0)
        qkv = jnp.dot(rows, weight[:, :384], preferred_element_type=F32)
        query = head_norm(qkv[:, :128], gain[0:1], half)
        key = head_norm(qkv[:, 128:256], gain[1:2], half)
        kv = jnp.concatenate([key, qkv[:, 256:].astype(BF16)], axis=1)
        for i in range(4):
            place = core if i < 2 else 1 - core
            row = pl.multiple_of(low * 512 + i % 2 * 256 + place * 128, 128)
            q_s[pl.ds(row, 128)] = query[i * 128 : i * 128 + 128]
            kv_s[pl.ds(pl.multiple_of(row + WIN, WIN), 128)] = kv[i * 128 : i * 128 + 128]
    for b in range(8):
        att[lax.rem(core + b, 2), b // 2] = attend(
            q_s[b * 128 : b * 128 + 128],
            kv_s[b * 128 : b * 128 + 256],
            first[b : b + 1],
            count[b : b + 1],
            anchor + (b * 128 - WIN),
        )
    keep[...] = att[0].reshape(512, 128)
    both[:512] = att[1].reshape(512, 128)
    both[512:] = weight[:, 384:]


def project_kernel(at, keep, sent, got, mine, away):
    y = at[0]
    rows = jnp.concatenate([keep[...], got[:512]], axis=1)
    weight = jnp.concatenate([sent[512:], got[512:]], axis=1)
    part = lax.dot_general(rows, weight, NT, preferred_element_type=F32)
    for t in range(4):
        block = part[t * 128 : t * 128 + 128]

        @pl.when(y == t)
        def _():
            mine[...] = block

        @pl.when(y != t)
        def _():
            away[lax.rem(t + 3 - y, 4)] = block.astype(BF16)


def middle_kernel(tok, mine, a, b, c, gain, middle, normed):
    total = mine[...] + a[...].astype(F32) + b[...].astype(F32) + c[...].astype(F32)
    mid = (tok[...].astype(F32) + total).astype(BF16)
    middle[...] = mid
    normed[...] = layer_norm(mid.astype(F32), gain[...])


def hidden_share(rows, weight):
    hidden = jax.nn.gelu(
        jnp.dot(rows, weight[:, :512], preferred_element_type=F32), approximate=True
    ).astype(BF16)
    return lax.dot_general(hidden, weight[:, 512:], NT, preferred_element_type=F32)


def mlp_first_kernel(a, b, c, weight, out):
    rows = jnp.concatenate([a[...], b[...], c[...]], axis=0)
    out[...] = hidden_share(rows, weight)


def mlp_second_kernel(a, b, c, weight, part, mine, to_b, to_c):
    rows = jnp.concatenate([a[...], b[...], c[...]], axis=0)
    total = part[...] + hidden_share(rows, weight)
    mine[...] = total[:128]
    to_b[...] = total[128:256].astype(BF16)
    to_c[...] = total[256:].astype(BF16)


def mlp_far_kernel(low, high, weight, other, out):
    rows = jnp.concatenate([low[...], high[...]], axis=0)
    out[...] = (hidden_share(rows, weight) + hidden_share(rows, other)).astype(BF16)


def end_kernel(middle, mine, a, b, c, out):
    total = middle[...].astype(F32) + mine[...]
    total += a[...].astype(F32) + b[...].astype(F32) + c[...].astype(F32)
    out[...] = total.astype(BF16)


def call(kernel, outs, specs, name, mib=8, scratch=(), flops=2**20, **more):
    return pl.pallas_call(
        kernel,
        out_shape=[jax.ShapeDtypeStruct(s, d) for s, d in outs],
        in_specs=specs,
        out_specs=[VMEM] * len(outs),
        scratch_shapes=list(scratch),
        compiler_params=params(mib),
        cost_estimate=pl.CostEstimate(flops=flops, bytes_accessed=2**21, transcendentals=0),
        name=name,
        **more,
    )


def fetch(value, axis, step):
    n = lax.axis_size(axis)
    return lax.ppermute(value, axis, [((i + step) % n, i) for i in range(n)])


def relay(block):
    half = block.shape[2] // 2
    right, left = fetch(block, "x", 1), fetch(block, "x", 3)
    far_low, far_high = fetch(right[:, :, :half], "x", 1), fetch(left[:, :, half:], "x", 3)
    return block, right, far_low, far_high, left


def local(
    tokens,
    win_first,
    win_count,
    norm1_gain,
    qkv_weight,
    qk_gain,
    out_weight,
    norm2_gain,
    up_weight,
    down_weight,
):
    y, core = lax.axis_index("y"), lax.axis_index("core")
    seq = lax.axis_index("z") * lax.axis_size("x") + lax.axis_index("x")
    at = jnp.stack([y, core, lax.axis_index("x"), seq * 1024]).astype(jnp.int32)
    first, count = win_first.reshape(8, 128), win_count.reshape(8, 128)

    (front,) = from_hbm(
        pack_kernel,
        [((8, 32, 512), BF16)],
        [jnp.transpose(qkv_weight, (1, 0, 2)), out_weight.T],
        "pack",
    )
    (normed,) = from_hbm(
        norm_kernel,
        [((128, 1024), BF16)],
        [tokens, norm1_gain.reshape(1, 1024)],
        "norm",
    )
    (back,) = from_hbm(
        mlp_pack_kernel,
        [((8, 32, 1024), BF16)],
        [up_weight, down_weight.T],
        "mlp_pack",
    )
    front = lax.all_to_all(front, "z", 0, 0, tiled=True)
    far = {k: fetch(normed, "y", k) for k in (1, 3, 2)}
    back, front = lax.optimization_barrier((back, front))
    weights = relay(front)
    back = lax.all_to_all(back, "z", 0, 0, tiled=True)
    far, _ = lax.optimization_barrier((far, (weights[1], weights[4])))
    own_low, own_high, border = call(
        collect_kernel,
        [((2, 128, 1024), BF16), ((2, 128, 1024), BF16), ((WIN, 1024), BF16)],
        [SMEM] + [VMEM] * 4,
        "collect",
    )(at, normed, far[1], far[2], far[3])
    peer_low, peer_high = fetch(own_low, "core", 1), fetch(own_high, "core", 1)
    spot = lambda z, x, y, core: ((z * 4 + x) * 4 + y) * 2 + core
    shift = lambda s, by: divmod((s + by) % 32, 4)
    near_own = lax.ppermute(
        border,
        ("z", "x", "y", "core"),
        [
            (spot(*divmod(s, 4), j, c), spot(*shift(s, 2 * c - 1), j, c))
            for s in range(32)
            for j in range(4)
            for c in range(2)
        ],
    )
    near_peer = fetch(near_own, "core", 1)
    keep, both = call(
        attention_kernel,
        [((512, 128), BF16), ((1536, 128), BF16)],
        [SMEM] + [VMEM] * 14,
        "attention",
        scratch=[
            pltpu.VMEM((1024, 512), BF16),
            pltpu.VMEM((1024, 128), BF16),
            pltpu.VMEM((1024 + 2 * WIN, 256), BF16),
            pltpu.VMEM((2, 4, 128, 128), BF16),
        ],
    )(at, own_low, own_high, peer_low, peer_high, *weights, near_own, near_peer, qk_gain, first, count)

    mlp_weights = relay(back)
    got = fetch(both, "core", 1)
    mine_attended, away = call(
        project_kernel,
        [((128, 1024), F32), ((3, 128, 1024), BF16)],
        [SMEM] + [VMEM] * 3,
        "project",
    )(at, keep, both, got)
    parts = [fetch(away[k - 1], "y", 4 - k) for k in (1, 3, 2)]
    middle, normed_two = call(
        middle_kernel,
        [((128, 1024), BF16)] * 2,
        [VMEM] * 6,
        "middle",
    )(tokens, mine_attended, *parts, norm2_gain.reshape(1, 1024))

    near = {k: fetch(normed_two, "y", k) for k in (1, 3)}
    (mlp_own,) = call(lay_kernel, [((1024, 1024), BF16)], [SMEM] + [VMEM] * 5, "mlp_lay")(
        at, *mlp_weights
    )
    mlp_own, near = lax.optimization_barrier((mlp_own, near))
    low, high = fetch(near[1][:64], "y", 1), fetch(near[3][64:], "y", 3)
    mlp_peer = fetch(mlp_own, "core", 1)
    (part,) = call(mlp_first_kernel, [((384, 1024), F32)], [VMEM] * 4, "mlp_first", mib=16)(
        normed_two, near[1], near[3], mlp_own
    )
    mine, to_right, to_left = call(
        mlp_second_kernel,
        [((128, 1024), F32)] + [((128, 1024), BF16)] * 2,
        [VMEM] * 5,
        "mlp_second",
        mib=16,
    )(normed_two, near[1], near[3], mlp_peer, part)
    parts = [fetch(to_right, "y", 3), fetch(to_left, "y", 1)]
    (low, high), mine = lax.optimization_barrier(((low, high), mine))
    (to_far,) = call(mlp_far_kernel, [((128, 1024), BF16)], [VMEM] * 4, "mlp_far", mib=16)(
        low, high, mlp_own, mlp_peer
    )
    parts.append(fetch(to_far, "y", 2))
    (out,) = call(end_kernel, [((128, 1024), BF16)], [VMEM] * 5, "end")(middle, mine, *parts)
    return out


def solution(mesh):
    fine = Mesh(mesh.devices.reshape(8, 4, 4, 2), ("z", "x", "y", "core"))
    seq, head = ("z", "x"), ("y", "core")
    return jax.shard_map(
        local,
        mesh=fine,
        in_specs=(
            P(seq + head, None),
            P(seq),
            P(seq),
            P(),
            P(seq, None, head),
            P(None, head, None),
            P(head, seq),
            P(),
            P(seq, head),
            P(head, seq),
        ),
        out_specs=P(seq + head, None),
        check_vma=False,
    )
```

```python
import jax
import jax.numpy as jnp
from jax import lax
from jax.experimental import pallas as pl
from jax.experimental.pallas import tpu as pltpu
from jax.sharding import Mesh, PartitionSpec as P

WIN = 64
F32, BF16 = jnp.float32, jnp.bfloat16
NT = (((1,), (1,)), ((), ()))
VMEM = pl.BlockSpec(memory_space=pltpu.VMEM)
HBM = pl.BlockSpec(memory_space=pltpu.HBM)
SMEM = pl.BlockSpec(memory_space=pltpu.SMEM)


def params(mib):
    return pltpu.CompilerParams(vmem_limit_bytes=mib * 2**20)


def layer_norm(values, gain):
    center = values - jnp.mean(values, axis=-1, keepdims=True)
    spread = jnp.mean(center * center, axis=-1, keepdims=True)
    return (center * lax.rsqrt(spread + 1e-06) * gain).astype(BF16)


def head_norm(values, gain, half):
    square = values * values
    low = jnp.sum(jnp.where(half, square, 0.0), axis=-1, keepdims=True)
    high = jnp.sum(jnp.where(half, 0.0, square), axis=-1, keepdims=True)
    scale = lax.rsqrt(jnp.where(half, low, high) * (1.0 / 64) + 1e-06)
    return (values * scale * gain).astype(BF16)


def first_half(rows):
    return lax.broadcasted_iota(jnp.int32, (rows, 128), 1) < 64


def bring(held, here, sems):
    copies = [
        pltpu.make_async_copy(a, b, sems.at[i]) for i, (a, b) in enumerate(zip(held, here))
    ]
    for copy in copies:
        copy.start()
    return copies


def pack_kernel(*refs):
    held, front, here, sems = refs[:2], refs[2], refs[3:5], refs[5]
    for copy in bring(held, here, sems):
        copy.wait()
    qkv, out_t = here
    pack = jnp.concatenate([qkv[0], qkv[1], qkv[2], out_t[...]], axis=1)
    for i in range(8):
        front[i] = pack


def norm_kernel(*refs):
    held, normed, here, sems = refs[:2], refs[2], refs[3:5], refs[5]
    for copy in bring(held, here, sems):
        copy.wait()
    tok, gain = here
    normed[...] = layer_norm(tok[...].astype(F32), gain[...])


def mlp_pack_kernel(*refs):
    held, back, here, sems = refs[:2], refs[2], refs[3:5], refs[5]
    for copy in bring(held, here, sems):
        copy.wait()
    up, down_t = here
    pack = jnp.concatenate([up[...], down_t[...]], axis=1)
    for i in range(8):
        back[i] = pack


def from_hbm(kernel, outs, given, name):
    return call(
        kernel,
        outs,
        [HBM] * len(given),
        name,
        scratch=[pltpu.VMEM(v.shape, v.dtype) for v in given]
        + [pltpu.SemaphoreType.DMA((len(given),))],
    )(*[pltpu.with_memory_space_constraint(v, pltpu.HBM) for v in given])


def collect_kernel(at, *refs):
    blocks, own, border = refs[:4], refs[4:6], refs[6]
    y, core = at[0], at[1]
    for k in range(4):
        t = lax.rem(y + k, 4)
        for low in range(2):

            @pl.when(t // 2 == low)
            def _():
                own[low][lax.rem(t, 2)] = blocks[k][...]

        @pl.when((core == 0) & (t == 0))
        def _():
            border[...] = blocks[k][:WIN]

        @pl.when((core == 1) & (t == 3))
        def _():
            border[...] = blocks[k][128 - WIN :]


def lay(x, here, right, far_low, far_high, left, out):
    half = out.shape[1] // 2
    for k, block in enumerate((here, right, None, left)):
        base = lax.rem(x + k, 4) * 32
        for z in range(8):
            rows = pl.ds(pl.multiple_of(z * 128 + base, 32), 32)
            if block is None:
                out[rows, :half] = far_low[z]
                out[rows, half:] = far_high[z]
            else:
                out[rows] = block[z]


def lay_kernel(at, *refs):
    lay(at[2], *refs)


def attend(query, kv, first, count, key_start):
    lower = jnp.broadcast_to(first, (128, 128)).T
    upper = lower + jnp.broadcast_to(count, (128, 128)).T
    index = key_start + lax.broadcasted_iota(jnp.int32, (128, 256), 1)
    lower = jnp.concatenate([lower, lower], axis=1)
    upper = jnp.concatenate([upper, upper], axis=1)
    allowed = (index >= lower) & (index < upper)
    low = first_half(128)
    values = kv[:, 128:]
    one, none = jnp.ones_like(values), jnp.zeros_like(query)
    pick = first_half(256)
    sums = []
    for h in range(2):
        own = low if h == 0 else ~low
        score = lax.dot_general(
            jnp.where(own, query, none), kv[:, :128], NT, preferred_element_type=F32
        )
        weight = jnp.where(allowed, jnp.exp(score * 0.125), 0.0).astype(BF16)
        held = jnp.where(pick if h == 0 else ~pick, values, one)
        sums.append(jnp.dot(weight, held, preferred_element_type=F32))
    mixed = jnp.where(low, sums[0], sums[1])
    total = pltpu.roll(jnp.where(low, sums[1], sums[0]), 64, 1)
    return (mixed / total).astype(BF16)


def attention_kernel(
    at, own_low, own_high, peer_low, peer_high, here, right, far_low, far_high, left,
    near_own, near_peer, gains, first, count, keep, both, weight, q_s, kv_s, att,
):
    lay(at[2], here, right, far_low, far_high, left, weight)
    core, anchor = at[1], at[3]
    gain = gains[...]
    gain = jnp.concatenate([gain[:, 0], gain[:, 1]], axis=1)

    rows = jnp.concatenate([near_own[...], near_peer[...]], axis=0)
    part = jnp.dot(rows, weight[:, 128:384], preferred_element_type=F32)
    key = head_norm(part[:, :128], gain[1:2], first_half(2 * WIN))
    kv = jnp.concatenate([key, part[:, 128:].astype(BF16)], axis=1)
    end = WIN + 1024
    kv_s[pl.ds(pl.multiple_of((1 - core) * end, WIN), WIN)] = kv[:WIN]
    kv_s[pl.ds(pl.multiple_of(core * end, WIN), WIN)] = kv[WIN:]

    half = first_half(512)
    for low, (own, peer) in enumerate(((own_low, peer_low), (own_high, peer_high))):
        rows = jnp.concatenate([own[0], own[1], peer[0], peer[1]], axis=0)
        qkv = jnp.dot(rows, weight[:, :384], preferred_element_type=F32)
        query = head_norm(qkv[:, :128], gain[0:1], half)
        key = head_norm(qkv[:, 128:256], gain[1:2], half)
        kv = jnp.concatenate([key, qkv[:, 256:].astype(BF16)], axis=1)
        for i in range(4):
            place = core if i < 2 else 1 - core
            row = pl.multiple_of(low * 512 + i % 2 * 256 + place * 128, 128)
            q_s[pl.ds(row, 128)] = query[i * 128 : i * 128 + 128]
            kv_s[pl.ds(pl.multiple_of(row + WIN, WIN), 128)] = kv[i * 128 : i * 128 + 128]
    for b in range(8):
        att[lax.rem(core + b, 2), b // 2] = attend(
            q_s[b * 128 : b * 128 + 128],
            kv_s[b * 128 : b * 128 + 256],
            first[b : b + 1],
            count[b : b + 1],
            anchor + (b * 128 - WIN),
        )
    keep[...] = att[0].reshape(512, 128)
    both[:512] = att[1].reshape(512, 128)
    both[512:] = weight[:, 384:]


def project_kernel(at, keep, sent, got, mine, away):
    y = at[0]
    rows = jnp.concatenate([keep[...], got[:512]], axis=1)
    weight = jnp.concatenate([sent[512:], got[512:]], axis=1)
    part = lax.dot_general(rows, weight, NT, preferred_element_type=F32)
    for t in range(4):
        block = part[t * 128 : t * 128 + 128]

        @pl.when(y == t)
        def _():
            mine[...] = block

        @pl.when(y != t)
        def _():
            away[lax.rem(t + 3 - y, 4)] = block.astype(BF16)


def middle_kernel(tok, mine, a, b, c, gain, middle, normed):
    total = mine[...] + a[...].astype(F32) + b[...].astype(F32) + c[...].astype(F32)
    mid = (tok[...].astype(F32) + total).astype(BF16)
    middle[...] = mid
    normed[...] = layer_norm(mid.astype(F32), gain[...])


def hidden_share(rows, weight):
    hidden = jax.nn.gelu(
        jnp.dot(rows, weight[:, :512], preferred_element_type=F32), approximate=True
    ).astype(BF16)
    return lax.dot_general(hidden, weight[:, 512:], NT, preferred_element_type=F32)


def mlp_first_kernel(a, b, c, weight, out):
    rows = jnp.concatenate([a[...], b[...], c[...]], axis=0)
    out[...] = hidden_share(rows, weight)


def mlp_second_kernel(a, b, c, weight, part, mine, to_b, to_c):
    rows = jnp.concatenate([a[...], b[...], c[...]], axis=0)
    total = part[...] + hidden_share(rows, weight)
    mine[...] = total[:128]
    to_b[...] = total[128:256].astype(BF16)
    to_c[...] = total[256:].astype(BF16)


def mlp_far_kernel(low, high, weight, other, to_low, to_high):
    rows = jnp.concatenate([low[...], high[...]], axis=0)
    total = (hidden_share(rows, weight) + hidden_share(rows, other)).astype(BF16)
    to_low[...] = total[:64]
    to_high[...] = total[64:]


def end_kernel(middle, mine, a, b, low, high, out):
    total = middle[...].astype(F32) + mine[...]
    total += a[...].astype(F32) + b[...].astype(F32)
    out[:64] = (total[:64] + low[...].astype(F32)).astype(BF16)
    out[64:] = (total[64:] + high[...].astype(F32)).astype(BF16)


def call(kernel, outs, specs, name, mib=8, scratch=(), flops=2**20, **more):
    return pl.pallas_call(
        kernel,
        out_shape=[jax.ShapeDtypeStruct(s, d) for s, d in outs],
        in_specs=specs,
        out_specs=[VMEM] * len(outs),
        scratch_shapes=list(scratch),
        compiler_params=params(mib),
        cost_estimate=pl.CostEstimate(flops=flops, bytes_accessed=2**21, transcendentals=0),
        name=name,
        **more,
    )


def fetch(value, axis, step):
    n = lax.axis_size(axis)
    return lax.ppermute(value, axis, [((i + step) % n, i) for i in range(n)])


def relay(block):
    half = block.shape[2] // 2
    right, left = fetch(block, "x", 1), fetch(block, "x", 3)
    far_low, far_high = fetch(right[:, :, :half], "x", 1), fetch(left[:, :, half:], "x", 3)
    return block, right, far_low, far_high, left


def local(
    tokens,
    win_first,
    win_count,
    norm1_gain,
    qkv_weight,
    qk_gain,
    out_weight,
    norm2_gain,
    up_weight,
    down_weight,
):
    y, core = lax.axis_index("y"), lax.axis_index("core")
    seq = lax.axis_index("z") * lax.axis_size("x") + lax.axis_index("x")
    at = jnp.stack([y, core, lax.axis_index("x"), seq * 1024]).astype(jnp.int32)
    first, count = win_first.reshape(8, 128), win_count.reshape(8, 128)

    (front,) = from_hbm(
        pack_kernel,
        [((8, 32, 512), BF16)],
        [jnp.transpose(qkv_weight, (1, 0, 2)), out_weight.T],
        "pack",
    )
    (normed,) = from_hbm(
        norm_kernel,
        [((128, 1024), BF16)],
        [tokens, norm1_gain.reshape(1, 1024)],
        "norm",
    )
    (back,) = from_hbm(
        mlp_pack_kernel,
        [((8, 32, 1024), BF16)],
        [up_weight, down_weight.T],
        "mlp_pack",
    )
    front = lax.all_to_all(front, "z", 0, 0, tiled=True)
    far = {k: fetch(normed, "y", k) for k in (1, 3, 2)}
    back, front = lax.optimization_barrier((back, front))
    weights = relay(front)
    back = lax.all_to_all(back, "z", 0, 0, tiled=True)
    far, _ = lax.optimization_barrier((far, (weights[1], weights[4])))
    own_low, own_high, border = call(
        collect_kernel,
        [((2, 128, 1024), BF16), ((2, 128, 1024), BF16), ((WIN, 1024), BF16)],
        [SMEM] + [VMEM] * 4,
        "collect",
    )(at, normed, far[1], far[2], far[3])
    peer_low, peer_high = fetch(own_low, "core", 1), fetch(own_high, "core", 1)
    spot = lambda z, x, y, core: ((z * 4 + x) * 4 + y) * 2 + core
    shift = lambda s, by: divmod((s + by) % 32, 4)
    near_own = lax.ppermute(
        border,
        ("z", "x", "y", "core"),
        [
            (spot(*divmod(s, 4), j, c), spot(*shift(s, 2 * c - 1), j, c))
            for s in range(32)
            for j in range(4)
            for c in range(2)
        ],
    )
    near_peer = fetch(near_own, "core", 1)
    keep, both = call(
        attention_kernel,
        [((512, 128), BF16), ((1536, 128), BF16)],
        [SMEM] + [VMEM] * 14,
        "attention",
        scratch=[
            pltpu.VMEM((1024, 512), BF16),
            pltpu.VMEM((1024, 128), BF16),
            pltpu.VMEM((1024 + 2 * WIN, 256), BF16),
            pltpu.VMEM((2, 4, 128, 128), BF16),
        ],
    )(at, own_low, own_high, peer_low, peer_high, *weights, near_own, near_peer, qk_gain, first, count)

    mlp_weights = relay(back)
    got = fetch(both, "core", 1)
    mine_attended, away = call(
        project_kernel,
        [((128, 1024), F32), ((3, 128, 1024), BF16)],
        [SMEM] + [VMEM] * 3,
        "project",
    )(at, keep, both, got)
    parts = [fetch(away[k - 1], "y", 4 - k) for k in (1, 3, 2)]
    middle, normed_two = call(
        middle_kernel,
        [((128, 1024), BF16)] * 2,
        [VMEM] * 6,
        "middle",
    )(tokens, mine_attended, *parts, norm2_gain.reshape(1, 1024))

    near = {k: fetch(normed_two, "y", k) for k in (1, 3)}
    (mlp_own,) = call(lay_kernel, [((1024, 1024), BF16)], [SMEM] + [VMEM] * 5, "mlp_lay")(
        at, *mlp_weights
    )
    mlp_own, near = lax.optimization_barrier((mlp_own, near))
    low, high = fetch(near[1][:64], "y", 1), fetch(near[3][64:], "y", 3)
    mlp_peer = fetch(mlp_own, "core", 1)
    (part,) = call(mlp_first_kernel, [((384, 1024), F32)], [VMEM] * 4, "mlp_first", mib=16)(
        normed_two, near[1], near[3], mlp_own
    )
    mine, to_right, to_left = call(
        mlp_second_kernel,
        [((128, 1024), F32)] + [((128, 1024), BF16)] * 2,
        [VMEM] * 5,
        "mlp_second",
        mib=16,
    )(normed_two, near[1], near[3], mlp_peer, part)
    parts = [fetch(to_right, "y", 3), fetch(to_left, "y", 1)]
    (low, high), mine = lax.optimization_barrier(((low, high), mine))
    to_far = call(mlp_far_kernel, [((64, 1024), BF16)] * 2, [VMEM] * 4, "mlp_far", mib=16)(
        low, high, mlp_own, mlp_peer
    )
    parts += [fetch(half, "y", 2) for half in to_far]
    (out,) = call(end_kernel, [((128, 1024), BF16)], [VMEM] * 6, "end")(middle, mine, *parts)
    return out


def solution(mesh):
    fine = Mesh(mesh.devices.reshape(8, 4, 4, 2), ("z", "x", "y", "core"))
    seq, head = ("z", "x"), ("y", "core")
    return jax.shard_map(
        local,
        mesh=fine,
        in_specs=(
            P(seq + head, None),
            P(seq),
            P(seq),
            P(),
            P(seq, None, head),
            P(None, head, None),
            P(head, seq),
            P(),
            P(seq, head),
            P(head, seq),
        ),
        out_specs=P(seq + head, None),
        check_vma=False,
    )
```
